512 devices in a mesh: grp: 2 (over y_hi), wide: 64 (over y_lo, z, core), narrow: 4 (over x).
Axes of the slice: x: 4, y: 4 (y_hi: 2, y_lo: 2; y = y_hi * 2 + y_lo), z: 16, core: 2. Of those that a mesh axis runs over, the one named last changes fastest.
Arguments:
- hidden: bfloat16 [2048, 3584], P('wide'), may hold values from -6 to 6
- routes: int32 [2048, 8], P('wide'), may hold values from 0 to 63, all different within a row; in each aligned block of 32 rows (0 to 31, 32 to 63, ...) at most 8 rows name the same one
- route_gates: float32 [2048, 8], P('wide'), may hold values from 0.05 to 1
- gate_proj: bfloat16 [64, 3584, 1024], P('wide', None, ('grp', 'narrow')), may hold values from -0.09375 to 0.09375
- up_proj: bfloat16 [64, 3584, 1024], P('wide', None, ('grp', 'narrow')), may hold values from -0.09375 to 0.09375
- down_proj: bfloat16 [64, 1024, 3584], P('wide', ('grp', 'narrow')), may hold values from -0.1875 to 0.1875
Outputs:
- mixed: bfloat16 [2048, 3584], P('wide', ('grp', 'narrow'))
The draws below stay inside these ranges and needn't reach their ends.
Inputs may be any that keep to these rules, and one draw needn't show every extreme that they name: Each request names 8 different experts; among the routes of the 32 requests of one index of wide no expert is named more than 8 times, and that count is reached.
All inputs are finite; a program needn't handle non-finite values.
Results may differ from the reference program's by a relative error of at most 0.017.
Values may be sent and summed in bfloat16 or wider, within the bound.
No kernel may reach another device: no remote copies, remote signals or barrier semaphores. Data moves between devices by JAX's collectives and lax.ppermute only.
A program may use at most 192 MiB of HBM per device.

```python
import math
import jax
import jax.numpy as jnp
import numpy as np
from jax import lax

D = 3584
HID = 1024
EXPERTS = 64
TOPK = 8
TOK_DEV = 32
CAP = 8
REQUESTS = 2048
N_GRP = 2
N_WIDE = 64
N_NARROW = 4


def steps_of(rng, shape, shards, least, top_value):
    factor_of = 1.0
    for axis_at, parts in shards:
        draws = jax.random.uniform(jax.random.fold_in(jax.random.fold_in(rng, 6), axis_at), (parts,), jnp.float32, least / len(shards), top_value / len(shards))
        factor_of = factor_of * jnp.repeat(jnp.exp(draws), shape[axis_at] // parts).reshape((-1,) + (1,) * (len(shape) - 1 - axis_at))
    return factor_of


def shared_out(stream_key, own, number, rows, count, top, most, slope):
    order = jax.random.permutation(stream_key, count)
    crowded, ordinary = portions_of(count, rows * top, most, slope, True), portions_of(count, rows * top, most, slope, False)
    places = jnp.arange(count)

    def named(tallies, offset_by):
        used = int((tallies > 0).sum())
        fixed = max(1, used // 4)
        passed = fixed + (places - fixed + offset_by * (used - fixed)) % max(1, count - fixed)
        return jnp.zeros((count,), jnp.int32).at[order[jnp.where(places < fixed, places, passed)]].set(jnp.asarray(tallies, jnp.int32))

    tallies = jnp.where(number % 4 == 0, named(crowded, number // 4), named(ordinary, number - number // 4 - 1))
    mixed = jax.random.permutation(jax.random.fold_in(own, 3), count)
    giver, receiver = mixed[0:count // 2 * 2:2], mixed[1:count // 2 * 2:2]
    room = jnp.minimum(tallies[giver] - 1, most - tallies[receiver]) // 2
    room = jnp.where((giver == order[0]) | (receiver == order[0]) | (tallies[receiver] == 0), 0, jnp.maximum(room, 0))
    passed = jax.random.randint(jax.random.fold_in(own, 4), (count // 2,), 0, 1 << 20) % (room + 1)
    tallies = tallies.at[giver].add(-passed).at[receiver].add(passed)
    items = jnp.searchsorted(jnp.cumsum(tallies), jnp.arange(rows * top), side="right").astype(jnp.int32)
    table = items.reshape(top, rows).T
    table = table[jax.random.permutation(jax.random.fold_in(own, 1), rows)]
    offset_by = jax.random.randint(jax.random.fold_in(own, 2), (rows, 1), 0, top)
    return jnp.take_along_axis(table, (jnp.arange(top)[None, :] + offset_by) % top, axis=1)


def portions_of(number_of, total, most, skew, full):
    loads = [(1 << 20) // math.isqrt(standing ** skew) + 1 for standing in range(1, number_of + 1)]
    largest = most if full else min(most, max(-(-total // number_of), total * loads[0] // sum(loads)))
    least = 1 if total - largest >= number_of - 1 else 0
    counts, rest = [largest] + [least] * (number_of - 1), total - largest - least * (number_of - 1)
    while rest > 0:
        candidates = [i for i in range(1, number_of) if counts[i] < largest] or [i for i in range(1, number_of) if counts[i] < most]
        mass, budget = sum([loads[i] for i in candidates]), rest
        for i in candidates:
            more = min(most - counts[i], max(1, budget * loads[i] // mass), rest)
            counts[i] = counts[i] + more
            rest = rest - more
    return np.array(counts)


def normal_values(stream_key, dims, width, limit, cuts=(), kind=jnp.bfloat16):
    values = jax.random.normal(stream_key, dims, jnp.float32) * width
    if len(cuts) > 0:
        values = steps_of(stream_key, dims, cuts, -0.22, 0.18) * values
    return jnp.clip(values, min=-limit, max=limit).astype(kind)


def setup_inputs(seed: int = 0) -> dict:
    arg_keys = jax.random.split(jax.random.key(seed), 7)
    hidden = normal_values(arg_keys[0], (REQUESTS, D), 1.0, 6.0, ((0, 64),))
    routes_keys = jax.random.split(jax.random.fold_in(arg_keys[1], 1), REQUESTS // TOK_DEV)
    routes_turns = jax.random.permutation(jax.random.fold_in(arg_keys[1], 3), REQUESTS // TOK_DEV)
    routes = jax.vmap(lambda own, number: shared_out(jax.random.fold_in(arg_keys[1], 2), own, number, TOK_DEV, EXPERTS, TOPK, CAP, 2))(routes_keys, routes_turns).reshape((REQUESTS, TOPK))
    route_gates = jnp.clip(jnp.exp(math.log(1.0) - 2.9957323 * jax.random.uniform(arg_keys[2], (REQUESTS, TOPK), jnp.float32) ** steps_of(arg_keys[2], (REQUESTS, TOPK), ((0, 64),), -0.2, 0.2)), 0.05, 1.0)
    gate_proj = normal_values(arg_keys[3], (EXPERTS, D, HID), D ** -0.5, 0.09375, ((0, 64), (2, 8)))
    up_proj = normal_values(arg_keys[4], (EXPERTS, D, HID), D ** -0.5, 0.09375, ((0, 64), (2, 8)))
    down_proj = normal_values(arg_keys[5], (EXPERTS, HID, D), HID ** -0.5, 0.1875, ((0, 64), (1, 8)))
    return dict(hidden=hidden, routes=routes, route_gates=route_gates, gate_proj=gate_proj, up_proj=up_proj, down_proj=down_proj)


def expert_rows(rows, w_gate, w_up, w_down):
    gate_act = jnp.dot(rows, w_gate, preferred_element_type=jnp.float32)
    up_act = jnp.dot(rows, w_up, preferred_element_type=jnp.float32)
    inner = (jax.nn.silu(gate_act) * up_act).astype(jnp.bfloat16)
    slices = N_GRP * N_NARROW
    slice_width = HID // slices
    inner3 = inner.reshape(rows.shape[0], slices, slice_width).astype(jnp.float32)
    down3 = w_down.reshape(slices, slice_width, D).astype(jnp.float32)
    pieces = jnp.einsum("rsh,shd->srd", inner3, down3)
    pieces = lax.optimization_barrier(pieces.astype(jnp.bfloat16)).astype(jnp.float32)
    return jnp.sum(pieces, axis=0)


def reference(hidden, routes, route_gates, gate_proj, up_proj, down_proj):
    total_rows = REQUESTS * TOPK
    route_flat = routes.reshape(-1).astype(jnp.int32)
    repeated = jnp.repeat(hidden, TOPK, axis=0)
    padded = jnp.concatenate([repeated, jnp.zeros((1, D), hidden.dtype)], axis=0)
    most_rows = N_WIDE * CAP

    def step(accum, item):
        w_gate, w_up, w_down, expert_id = item
        chosen = jnp.nonzero(route_flat == expert_id, size=most_rows, fill_value=total_rows)[0]
        result = expert_rows(padded[chosen], w_gate, w_up, w_down)
        return accum.at[chosen].add(result), None

    start = jnp.zeros((total_rows + 1, D), jnp.float32)
    expert_ids = jnp.arange(EXPERTS, dtype=jnp.int32)
    accum, _ = lax.scan(step, start, (gate_proj, up_proj, down_proj, expert_ids))
    outputs = accum[:total_rows].reshape(REQUESTS, TOPK, D)
    mixed = jnp.sum(outputs * route_gates[:, :, None], axis=1)
    return mixed.astype(jnp.bfloat16)
```

```python
import jax
import jax.numpy as jnp
from jax import lax
from jax.sharding import PartitionSpec as P

EXPERTS = 64
CAP = 8
F32 = jnp.float32
BF16 = jnp.bfloat16


def exchange(x, axis):
    return lax.all_to_all(x, axis, split_axis=0, concat_axis=0, tiled=True)


def per_device(hidden, routes, route_gates, gate_proj, up_proj, down_proj):
    tok, width = hidden.shape
    n_grp, n_nar = lax.axis_size("grp"), lax.axis_size("narrow")
    g, n = lax.axis_index("grp"), lax.axis_index("narrow")
    units = gate_proj.shape[2]
    part = width // (n_grp * n_nar)
    slots = EXPERTS * CAP

    gate_up = jnp.concatenate([gate_proj[0], up_proj[0]], axis=1).reshape(n_nar, n_grp, part, 2 * units)
    down = down_proj[0].reshape(units, n_grp, n_nar, part)
    gu_parts, down_parts = [], []
    for k in range(n_nar):
        to = lax.rem(n + k, n_nar)
        gu = lax.dynamic_index_in_dim(gate_up, to, 0, keepdims=False)
        dn = lax.dynamic_index_in_dim(down, to, 2, keepdims=False)
        if k:
            pairs = [(i, (i + k) % n_nar) for i in range(n_nar)]
            gu = lax.ppermute(gu, "narrow", pairs)
            dn = lax.ppermute(dn, "narrow", pairs)
        gu_parts.append(gu)
        down_parts.append(dn)

    experts = lax.broadcasted_iota(jnp.int32, (EXPERTS, 1, 1), 0)
    match = routes.T[None] == experts
    chosen = jnp.any(match, axis=1)
    gates = jnp.sum(jnp.where(match, route_gates.T[None], 0.0), axis=1)
    before = (
        lax.broadcasted_iota(jnp.int32, (tok, tok), 0) < lax.broadcasted_iota(jnp.int32, (tok, tok), 1)
    ).astype(BF16)
    place = jnp.dot(chosen.astype(BF16), before, preferred_element_type=F32)
    slot = lax.broadcasted_iota(jnp.int32, (1, CAP, 1), 1).astype(F32)
    picked = (place[:, None] == slot) & chosen[:, None]
    picker = picked.astype(BF16).reshape(slots, tok)
    weight = jnp.where(picked, gates[:, None], 0.0).reshape(slots, tok)
    weight_hi = weight.astype(BF16)
    weight_lo = (weight - weight_hi.astype(F32)).astype(BF16)
    weights = jnp.concatenate([weight_hi, weight_lo], axis=1)

    mine = lax.dynamic_slice_in_dim(hidden, (n * n_grp + g) * part, part, 1)
    outgoing = jnp.dot(picker, mine, preferred_element_type=F32).astype(BF16)
    rows = exchange(outgoing.reshape(EXPERTS, CAP, part), "wide").reshape(1, slots, part)
    rows = exchange(jnp.broadcast_to(rows, (n_grp, slots, part)), "grp")

    acts = jnp.zeros((n_nar, slots, 2 * units), BF16)
    for k in range(n_nar):
        act = sum(jnp.dot(rows[i], gu_parts[k][i], preferred_element_type=F32) for i in range(n_grp))
        acts = lax.dynamic_update_index_in_dim(acts, act.astype(BF16), lax.rem(n - k + n_nar, n_nar), 0)
    act = jnp.sum(exchange(acts, "narrow").astype(F32), axis=0)
    inner = (jax.nn.silu(act[:, :units]) * act[:, units:]).astype(BF16)
    inners = exchange(jnp.broadcast_to(inner[None], (n_nar, slots, units)), "narrow")

    outs = []
    for i in range(n_grp):
        out = 0.0
        for k in range(n_nar):
            left = lax.dynamic_index_in_dim(inners, lax.rem(n - k + n_nar, n_nar), 0, keepdims=False)
            out = out + jnp.dot(left, down_parts[k][:, i], preferred_element_type=F32)
        outs.append(out.astype(BF16))
    out = jnp.sum(exchange(jnp.stack(outs), "grp").astype(F32), axis=0).astype(BF16)
    back = exchange(out.reshape(EXPERTS, CAP, part), "wide").reshape(slots, part)
    mixed = lax.dot_general(weights, back, (((0,), (0,)), ((), ())), preferred_element_type=F32)
    return (mixed[:tok] + mixed[tok:]).astype(BF16)


def solution(mesh):
    return jax.shard_map(
        per_device,
        mesh=mesh,
        in_specs=(
            P("wide", None),
            P("wide", None),
            P("wide", None),
            P("wide", None, ("grp", "narrow")),
            P("wide", None, ("grp", "narrow")),
            P("wide", ("grp", "narrow"), None),
        ),
        out_specs=P("wide", ("grp", "narrow")),
        check_vma=False,
    )
```

```python
import functools

import jax
import jax.numpy as jnp
from jax import lax
from jax.experimental import pallas as pl
from jax.experimental.pallas import tpu as pltpu
from jax.sharding import Mesh, PartitionSpec as P

CAP = 8
F32 = jnp.float32
BF16 = jnp.bfloat16
I32 = jnp.int32
FAR = "zfar"
NEAR = ("grp", "ylo", "znear", "core")
AXES = ("grp", "ylo", "zfar", "znear", "core", "narrow")
WIDE = ("ylo", "zfar", "znear", "core")
LANES = 512

VMEM = pl.BlockSpec(memory_space=pltpu.VMEM)
SMEM = pl.BlockSpec(memory_space=pltpu.SMEM)
ANY = pl.BlockSpec(memory_space=pl.ANY)


def call(body, outs, specs, args, flops=0):
    single = not isinstance(outs, list)
    outs = [outs] if single else outs
    nbytes = sum(a.size * a.dtype.itemsize for a in args) + sum(o.size * o.dtype.itemsize for o in outs)
    got = pl.pallas_call(
        body,
        out_shape=outs,
        in_specs=specs,
        out_specs=[VMEM] * len(outs),
        compiler_params=pltpu.CompilerParams(vmem_limit_bytes=40 * 1024 * 1024),
        cost_estimate=pl.CostEstimate(flops=flops, bytes_accessed=nbytes, transcendentals=0),
    )(*args)
    return got[0] if single else got


def exchange(x, axis):
    return lax.all_to_all(x, axis, split_axis=0, concat_axis=0, tiled=True)


def pick_body(part, top, far_ref, rows_ref, *rest):
    out_ref, weight_ref = rest[-2:]
    blocks, tok, _ = rows_ref.shape
    count = blocks * tok
    rows = rows_ref[...].reshape(count, LANES)
    extra = rows[:, part : part + 3 * top]
    eye = (
        lax.broadcasted_iota(I32, (3 * top, 3 * top), 0) == lax.broadcasted_iota(I32, (3 * top, 3 * top), 1)
    ).astype(BF16)
    extra = lax.dot_general(eye, extra, (((1,), (1,)), ((), ())), preferred_element_type=F32)
    j = lax.broadcasted_iota(I32, (8, count), 0)
    z_count = 2 * lax.axis_size(FAR)
    expert = (((j // 4) * z_count + far_ref[0] * 2 + (j // 2) % 2) * 2 + j % 2).astype(F32)
    chosen = jnp.zeros((8, count), F32)
    gate = jnp.zeros((8, count), F32)
    for k in range(top):
        same = extra[k : k + 1] == expert
        chosen = jnp.where(same, 1.0, chosen)
        value = extra[top + k : top + k + 1] + extra[2 * top + k : 2 * top + k + 1]
        gate = gate + jnp.where(same, value, 0.0)
    first = lax.broadcasted_iota(I32, (count, count), 0)
    second = lax.broadcasted_iota(I32, (count, count), 1)
    before = ((first < second) & (first // tok == second // tok)).astype(BF16)
    place = jnp.dot(chosen.astype(BF16), before, preferred_element_type=F32)
    block = (lax.broadcasted_iota(I32, (8, count), 1) // tok).astype(F32)
    slot = jnp.where(chosen > 0.0, place + block * CAP, -1.0)
    want = lax.broadcasted_iota(I32, (8, blocks * CAP, count), 1).astype(F32)
    hit = slot[:, None, :] == want
    picker = jnp.where(hit, 1.0, 0.0).astype(BF16).reshape(8 * blocks * CAP, count)
    weight = jnp.where(hit, gate[:, None, :], 0.0).reshape(8 * blocks * CAP, count)
    high = weight.astype(BF16)
    weight_ref[:, :count] = high
    weight_ref[:, count:] = (weight - high.astype(F32)).astype(BF16)
    got = jnp.dot(picker, rows[:, :part], preferred_element_type=F32).astype(BF16)
    got = got.reshape(8, blocks * CAP, part)
    out_ref[:8] = got
    out_ref[8:] = got


def gate_up_body(n_nar, me_ref, rows_ref, *rest):
    parts, out_ref = rest[:n_nar], rest[-1]
    slots, part = out_ref.shape[1], rows_ref.shape[2]
    half = rows_ref.shape[0] // 2
    left = rows_ref[:half].reshape(slots, part)
    right = rows_ref[half:].reshape(slots, part)
    for k in range(n_nar):
        act = jnp.dot(left, parts[k][0], preferred_element_type=F32)
        act = act + jnp.dot(right, parts[k][1], preferred_element_type=F32)
        out_ref[lax.rem(me_ref[0] - k + n_nar, n_nar)] = act.astype(BF16)


def inner_body(acts_ref, out_ref):
    count, _, units = out_ref.shape
    act = sum(acts_ref[i].astype(F32) for i in range(count))
    gate, up = act[:, :units], act[:, units:]
    inner = (gate / (1.0 + jnp.exp(-gate)) * up).astype(BF16)
    for i in range(count):
        out_ref[i] = inner


def down_body(n_nar, me_ref, inner_ref, *rest):
    parts, out_ref = rest[:n_nar], rest[-1]
    half = out_ref.shape[0] // 2
    for i in range(2):
        out = 0.0
        for k in range(n_nar):
            left = inner_ref[lax.rem(me_ref[0] - k + n_nar, n_nar)]
            out = out + jnp.dot(left, parts[k][i], preferred_element_type=F32)
        out = out.astype(BF16)
        out_ref[i * half : (i + 1) * half] = out.reshape(half, -1, out.shape[1])


def combine_body(rows_ref, weight_ref, out_ref):
    blocks, tok, part = out_ref.shape
    half = rows_ref.shape[0] // 2
    weight = weight_ref[...]
    total = 0.0
    for i in range(2):
        rows = rows_ref[i * half : (i + 1) * half].reshape(weight.shape[0], part)
        total = total + lax.dot_general(weight, rows, (((0,), (0,)), ((), ())), preferred_element_type=F32)
    count = blocks * tok
    out_ref[...] = (total[:count] + total[count:]).astype(BF16).reshape(blocks, tok, part)


def per_device(hidden, routes, route_gates, gate_proj, up_proj, down_proj):
    tok, width = hidden.shape
    top = routes.shape[1]
    n_grp, n_nar, n_far = lax.axis_size("grp"), lax.axis_size("narrow"), lax.axis_size(FAR)
    g, n = lax.axis_index("grp"), lax.axis_index("narrow")
    me = n.astype(I32).reshape(1)
    far = lax.axis_index(FAR).astype(I32).reshape(1)
    units = gate_proj.shape[2]
    part = width // (n_grp * n_nar)
    near = 16
    slots = 8 * n_far * CAP

    mine = lax.dynamic_slice_in_dim(hidden, (n * n_grp + g) * part, part, 1)
    gate_hi = route_gates.astype(BF16)
    gate_lo = (route_gates - gate_hi.astype(F32)).astype(BF16)
    spare = jnp.zeros((tok, LANES - part - 3 * top), BF16)
    rows = jnp.concatenate([mine, routes.astype(BF16), gate_hi, gate_lo, spare], axis=1)
    rows = exchange(jnp.broadcast_to(rows[None], (n_far, tok, LANES)), FAR)

    gate_up = jnp.concatenate([gate_proj[0], up_proj[0]], axis=1).reshape(n_nar, n_grp, part, 2 * units)
    down = down_proj[0].reshape(units, n_grp, n_nar, part).transpose(2, 1, 0, 3)
    gu_parts, down_parts = [], []
    for k in range(n_nar):
        to = lax.rem(n + k, n_nar)
        gu = lax.dynamic_index_in_dim(gate_up, to, 0, keepdims=False)
        dn = lax.dynamic_index_in_dim(down, to, 0, keepdims=False)
        if k:
            pairs = [(i, (i + k) % n_nar) for i in range(n_nar)]
            gu = lax.ppermute(gu, "narrow", pairs)
            dn = lax.ppermute(dn, "narrow", pairs)
        gu_parts.append(gu)
        down_parts.append(dn)

    picked, weight = call(
        functools.partial(pick_body, part, top),
        [
            jax.ShapeDtypeStruct((near, n_far * CAP, part), BF16),
            jax.ShapeDtypeStruct((slots, 2 * n_far * tok), BF16),
        ],
        [SMEM, VMEM] + [ANY] * (n_nar - 1),
        [far, rows] + gu_parts[1:],
        flops=2 * slots * n_far * tok * part,
    )
    rows = exchange(picked, NEAR)

    acts = call(
        functools.partial(gate_up_body, n_nar),
        jax.ShapeDtypeStruct((n_nar, slots, 2 * units), BF16),
        [SMEM, VMEM] + [VMEM] * n_nar + [ANY] * (n_nar - 1),
        [me, rows] + gu_parts + down_parts[1:],
        flops=2 * slots * part * 2 * units * 2 * n_nar,
    )
    acts = exchange(acts, "narrow")
    inner = call(inner_body, jax.ShapeDtypeStruct((n_nar, slots, units), BF16), [VMEM], [acts])
    inner = exchange(inner, "narrow")
    outs = call(
        functools.partial(down_body, n_nar),
        jax.ShapeDtypeStruct((near, n_far * CAP, part), BF16),
        [SMEM, VMEM] + [VMEM] * n_nar,
        [me, inner] + down_parts,
        flops=2 * slots * units * n_nar * 2 * part,
    )
    outs = exchange(outs, NEAR)
    sums = call(
        combine_body,
        jax.ShapeDtypeStruct((n_far, tok, part), BF16),
        [VMEM, VMEM],
        [outs, weight],
        flops=2 * slots * 2 * 2 * n_far * tok * part,
    )
    sums = exchange(sums, FAR)
    return jnp.sum(sums.astype(F32), axis=0).astype(BF16)


def solution(mesh):
    n_grp, n_wide, n_nar = mesh.devices.shape
    fine = Mesh(mesh.devices.reshape(n_grp, 2, n_wide // 8, 2, 2, n_nar), AXES)
    return jax.shard_map(
        per_device,
        mesh=fine,
        in_specs=(
            P(WIDE, None),
            P(WIDE, None),
            P(WIDE, None),
            P(WIDE, None, ("grp", "narrow")),
            P(WIDE, None, ("grp", "narrow")),
            P(WIDE, ("grp", "narrow"), None),
        ),
        out_specs=P(WIDE, ("grp", "narrow")),
        check_vma=False,
    )
```

```python
import functools

import jax
import jax.numpy as jnp
from jax import lax
from jax.experimental import pallas as pl
from jax.experimental.pallas import tpu as pltpu
from jax.sharding import Mesh, PartitionSpec as P

CAP = 8
F32 = jnp.float32
BF16 = jnp.bfloat16
I32 = jnp.int32
FAR = "zfar"
NEAR = ("grp", "ylo", "znear", "core")
AXES = ("grp", "ylo", "zfar", "znear", "core", "narrow")
WIDE = ("ylo", "zfar", "znear", "core")
LANES = 512

VMEM = pl.BlockSpec(memory_space=pltpu.VMEM)
SMEM = pl.BlockSpec(memory_space=pltpu.SMEM)
ANY = pl.BlockSpec(memory_space=pl.ANY)


def call(body, outs, specs, args, flops=0, scratch=()):
    single = not isinstance(outs, list)
    outs = [outs] if single else outs
    nbytes = sum(a.size * a.dtype.itemsize for a in args) + sum(o.size * o.dtype.itemsize for o in outs)
    got = pl.pallas_call(
        body,
        out_shape=outs,
        in_specs=specs,
        out_specs=[VMEM] * len(outs),
        scratch_shapes=list(scratch),
        compiler_params=pltpu.CompilerParams(vmem_limit_bytes=16 * 1024 * 1024),
        cost_estimate=pl.CostEstimate(flops=flops, bytes_accessed=nbytes, transcendentals=0),
    )(*args)
    return got[0] if single else got


def exchange(x, axis):
    return lax.all_to_all(x, axis, split_axis=0, concat_axis=0, tiled=True)


def rows_body(part, top, at_ref, hidden_ref, routes_ref, gates_ref, out_ref):
    count, tok, lanes = out_ref.shape
    odd = at_ref[1]
    start = pl.multiple_of(at_ref[0] * 2 * part + odd * (part // 128 * 128), 128)
    wide = hidden_ref[:, pl.ds(start, LANES)].astype(F32)
    mine = jnp.where(odd == 1, wide[:, LANES - part :], wide[:, :part])
    gates = gates_ref[...]
    high = gates.astype(BF16).astype(F32)
    extra = jnp.concatenate([routes_ref[...].astype(F32), high, gates - high], axis=0).astype(BF16)
    eye = (lax.broadcasted_iota(I32, (tok, tok), 0) == lax.broadcasted_iota(I32, (tok, tok), 1)).astype(BF16)
    extra = lax.dot_general(eye, extra, (((1,), (1,)), ((), ())), preferred_element_type=F32)
    spare = jnp.zeros((tok, lanes - part - 3 * top), F32)
    rows = jnp.concatenate([mine, extra, spare], axis=1).astype(BF16)
    for i in range(count):
        out_ref[i] = rows


def pack_body(n_nar, part, at_ref, gate_ref, up_ref, down_ref, *rest):
    outs, turned_ref = rest[:n_nar], rest[-1]
    units = gate_ref.shape[2]
    turned_ref[...] = jnp.transpose(down_ref[0])
    for k in range(n_nar):
        to = lax.rem(at_ref[0] + k, n_nar)
        for i in range(2):
            rows = pl.ds(pl.multiple_of((to * 2 + i) * part, 64), part)
            outs[k][i, :, :units] = gate_ref[0, rows]
            outs[k][i, :, units:] = up_ref[0, rows]
            rows = pl.ds(pl.multiple_of((i * n_nar + to) * part, 64), part)
            outs[k][2, :, i * units : (i + 1) * units] = turned_ref[rows]


def pick_body(part, top, far_ref, rows_ref, *rest):
    out_ref, weight_ref = rest[-2:]
    blocks, tok, _ = rows_ref.shape
    count = blocks * tok
    rows = rows_ref[...].reshape(count, LANES)
    extra = rows[:, part : part + 3 * top]
    eye = (
        lax.broadcasted_iota(I32, (3 * top, 3 * top), 0) == lax.broadcasted_iota(I32, (3 * top, 3 * top), 1)
    ).astype(BF16)
    extra = lax.dot_general(eye, extra, (((1,), (1,)), ((), ())), preferred_element_type=F32)
    j = lax.broadcasted_iota(I32, (8, count), 0)
    z_count = 2 * lax.axis_size(FAR)
    expert = (((j // 4) * z_count + far_ref[0] * 2 + (j // 2) % 2) * 2 + j % 2).astype(F32)
    chosen = jnp.zeros((8, count), F32)
    gate = jnp.zeros((8, count), F32)
    for k in range(top):
        same = extra[k : k + 1] == expert
        chosen = jnp.where(same, 1.0, chosen)
        value = extra[top + k : top + k + 1] + extra[2 * top + k : 2 * top + k + 1]
        gate = gate + jnp.where(same, value, 0.0)
    first = lax.broadcasted_iota(I32, (count, count), 0)
    second = lax.broadcasted_iota(I32, (count, count), 1)
    before = ((first < second) & (first // tok == second // tok)).astype(BF16)
    place = jnp.dot(chosen.astype(BF16), before, preferred_element_type=F32)
    block = (lax.broadcasted_iota(I32, (8, count), 1) // tok).astype(F32)
    slot = jnp.where(chosen > 0.0, place + block * CAP, -1.0)
    want = lax.broadcasted_iota(I32, (8, blocks * CAP, count), 1).astype(F32)
    hit = slot[:, None, :] == want
    picker = jnp.where(hit, 1.0, 0.0).astype(BF16).reshape(8 * blocks * CAP, count)
    weight = jnp.where(hit, gate[:, None, :], 0.0).reshape(8 * blocks * CAP, count)
    high = weight.astype(BF16)
    weight_ref[:, :count] = high
    weight_ref[:, count:] = (weight - high.astype(F32)).astype(BF16)
    got = jnp.dot(picker, rows[:, :part], preferred_element_type=F32).astype(BF16)
    got = got.reshape(8, blocks * CAP, part)
    out_ref[:8] = got
    out_ref[8:] = got


def gate_up_body(n_nar, me_ref, rows_ref, *rest):
    parts, out_ref = rest[:n_nar], rest[-1]
    slots, part = out_ref.shape[1], rows_ref.shape[2]
    half = rows_ref.shape[0] // 2
    left = rows_ref[:half].reshape(slots, part)
    right = rows_ref[half:].reshape(slots, part)
    for k in range(n_nar):
        act = jnp.dot(left, parts[k][0], preferred_element_type=F32)
        act = act + jnp.dot(right, parts[k][1], preferred_element_type=F32)
        out_ref[lax.rem(me_ref[0] - k + n_nar, n_nar)] = act.astype(BF16)


def inner_body(acts_ref, out_ref):
    count, _, units = out_ref.shape
    act = sum(acts_ref[i].astype(F32) for i in range(count))
    gate, up = act[:, :units], act[:, units:]
    inner = (gate / (1.0 + jnp.exp(-gate)) * up).astype(BF16)
    for i in range(count):
        out_ref[i] = inner


def down_body(n_nar, me_ref, inner_ref, *rest):
    parts, out_ref = rest[:n_nar], rest[-1]
    half = out_ref.shape[0] // 2
    units = inner_ref.shape[2]
    left = jnp.concatenate([inner_ref[lax.rem(me_ref[0] - k + n_nar, n_nar)] for k in range(n_nar)], axis=1)
    for i in range(2):
        right = jnp.concatenate([parts[k][2, :, i * units : (i + 1) * units] for k in range(n_nar)], axis=1)
        out = lax.dot_general(left, right, (((1,), (1,)), ((), ())), preferred_element_type=F32).astype(BF16)
        out_ref[i * half : (i + 1) * half] = out.reshape(half, -1, out.shape[1])


def combine_body(rows_ref, weight_ref, out_ref):
    blocks, tok, part = out_ref.shape
    half = rows_ref.shape[0] // 2
    weight = weight_ref[...]
    total = 0.0
    for i in range(2):
        rows = rows_ref[i * half : (i + 1) * half].reshape(weight.shape[0], part)
        total = total + lax.dot_general(weight, rows, (((0,), (0,)), ((), ())), preferred_element_type=F32)
    count = blocks * tok
    out_ref[...] = (total[:count] + total[count:]).astype(BF16).reshape(blocks, tok, part)


def per_device(hidden, routes, route_gates, gate_proj, up_proj, down_proj):
    tok, width = hidden.shape
    top = routes.shape[1]
    n_grp, n_nar, n_far = lax.axis_size("grp"), lax.axis_size("narrow"), lax.axis_size(FAR)
    g, n = lax.axis_index("grp"), lax.axis_index("narrow")
    far = lax.axis_index(FAR).astype(I32).reshape(1)
    units = gate_proj.shape[2]
    part = width // (n_grp * n_nar)
    near = 16
    slots = 8 * n_far * CAP

    at = jnp.stack([n, g]).astype(I32)
    rows = call(
        functools.partial(rows_body, part, top),
        jax.ShapeDtypeStruct((n_far, tok, LANES), BF16),
        [SMEM, VMEM, VMEM, VMEM],
        [at, hidden, routes.T, route_gates.T],
    )
    rows = exchange(rows, FAR)

    parts = call(
        functools.partial(pack_body, n_nar, part),
        [jax.ShapeDtypeStruct((3, part, 2 * units), BF16)] * n_nar,
        [SMEM, VMEM, VMEM, VMEM],
        [at, gate_proj, up_proj, down_proj],
        scratch=[pltpu.VMEM((width, units), BF16)],
    )
    parts = list(parts)
    for k in range(1, n_nar):
        parts[k] = lax.ppermute(parts[k], "narrow", [(i, (i + k) % n_nar) for i in range(n_nar)])
    sides = [parts[1], parts[-1]]

    picked, weight = call(
        functools.partial(pick_body, part, top),
        [
            jax.ShapeDtypeStruct((near, n_far * CAP, part), BF16),
            jax.ShapeDtypeStruct((slots, 2 * n_far * tok), BF16),
        ],
        [SMEM, VMEM] + [ANY] * 2,
        [far, rows] + sides,
        flops=2 * slots * n_far * tok * part,
    )
    rows = exchange(picked, NEAR)

    acts = call(
        functools.partial(gate_up_body, n_nar),
        jax.ShapeDtypeStruct((n_nar, slots, 2 * units), BF16),
        [SMEM, VMEM] + [VMEM] * n_nar,
        [at, rows] + parts,
        flops=2 * slots * part * 2 * units * 2 * n_nar,
    )
    acts = exchange(acts, "narrow")
    inner = call(inner_body, jax.ShapeDtypeStruct((n_nar, slots, units), BF16), [VMEM], [acts])
    inner = exchange(inner, "narrow")
    outs = call(
        functools.partial(down_body, n_nar),
        jax.ShapeDtypeStruct((near, n_far * CAP, part), BF16),
        [SMEM, VMEM] + [VMEM] * n_nar,
        [at, inner] + parts,
        flops=2 * slots * units * n_nar * 2 * part,
    )
    outs = exchange(outs, NEAR)
    sums = call(
        combine_body,
        jax.ShapeDtypeStruct((n_far, tok, part), BF16),
        [VMEM, VMEM],
        [outs, weight],
        flops=2 * slots * 2 * 2 * n_far * tok * part,
    )
    sums = exchange(sums, FAR)
    return jnp.sum(sums.astype(F32), axis=0).astype(BF16)


def solution(mesh):
    n_grp, n_wide, n_nar = mesh.devices.shape
    fine = Mesh(mesh.devices.reshape(n_grp, 2, n_wide // 8, 2, 2, n_nar), AXES)
    return jax.shard_map(
        per_device,
        mesh=fine,
        in_specs=(
            P(WIDE, None),
            P(WIDE, None),
            P(WIDE, None),
            P(WIDE, None, ("grp", "narrow")),
            P(WIDE, None, ("grp", "narrow")),
            P(WIDE, ("grp", "narrow"), None),
        ),
        out_specs=P(WIDE, ("grp", "narrow")),
        check_vma=False,
    )
```

```python
import functools

import jax
import jax.numpy as jnp
from jax import lax
from jax.experimental import pallas as pl
from jax.experimental.pallas import tpu as pltpu
from jax.sharding import Mesh, PartitionSpec as P

CAP = 8
F32 = jnp.float32
BF16 = jnp.bfloat16
I32 = jnp.int32
FAR = "zfar"
NEAR = ("grp", "ylo", "znear", "core")
AXES = ("grp", "ylo", "zfar", "znear", "core", "narrow")
WIDE = ("ylo", "zfar", "znear", "core")
LANES = 512
HOLD = 200 * 10**9

VMEM = pl.BlockSpec(memory_space=pltpu.VMEM)
SMEM = pl.BlockSpec(memory_space=pltpu.SMEM)
ANY = pl.BlockSpec(memory_space=pl.ANY)
HBM = pl.BlockSpec(memory_space=pltpu.HBM)


def call(body, outs, specs, args, flops=0, scratch=(), mib=16):
    single = not isinstance(outs, list)
    outs = [outs] if single else outs
    nbytes = sum(a.size * a.dtype.itemsize for a in args) + sum(o.size * o.dtype.itemsize for o in outs)
    got = pl.pallas_call(
        body,
        out_shape=outs,
        in_specs=specs,
        out_specs=[VMEM] * len(outs),
        scratch_shapes=list(scratch),
        compiler_params=pltpu.CompilerParams(vmem_limit_bytes=mib * 1024 * 1024),
        cost_estimate=pl.CostEstimate(flops=flops, bytes_accessed=nbytes, transcendentals=0),
    )(*args)
    return got[0] if single else got


def exchange(x, axis):
    return lax.all_to_all(x, axis, split_axis=0, concat_axis=0, tiled=True)


def rows_body(part, top, at_ref, hidden_hbm, routes_hbm, gates_hbm, out_ref, wide_ref, routes_ref, gates_ref, sems):
    count, tok, lanes = out_ref.shape
    odd = at_ref[1]
    start = pl.multiple_of(at_ref[0] * 2 * part + odd * (part // 128 * 128), 128)
    copies = [
        pltpu.make_async_copy(hidden_hbm.at[:, pl.ds(start, LANES)], wide_ref, sems.at[0]),
        pltpu.make_async_copy(routes_hbm, routes_ref, sems.at[1]),
        pltpu.make_async_copy(gates_hbm, gates_ref, sems.at[2]),
    ]
    for copy in copies:
        copy.start()
    for copy in copies:
        copy.wait()
    wide = wide_ref[...].astype(F32)
    mine = jnp.where(odd == 1, wide[:, LANES - part :], wide[:, :part])
    gates = gates_ref[...]
    high = gates.astype(BF16).astype(F32)
    extra = jnp.concatenate([routes_ref[...].astype(F32), high, gates - high], axis=0).astype(BF16)
    eye = (lax.broadcasted_iota(I32, (tok, tok), 0) == lax.broadcasted_iota(I32, (tok, tok), 1)).astype(BF16)
    extra = lax.dot_general(eye, extra, (((1,), (1,)), ((), ())), preferred_element_type=F32)
    spare = jnp.zeros((tok, lanes - part - 3 * top), F32)
    rows = jnp.concatenate([mine, extra, spare], axis=1).astype(BF16)
    for i in range(count):
        out_ref[i] = rows


def pack_body(n_nar, part, at_ref, gate_hbm, up_hbm, down_hbm, *rest):
    outs, (down_ref, turned_ref, sems, down_sem) = rest[:n_nar], rest[n_nar:]
    units = gate_hbm.shape[2]
    fetch = pltpu.make_async_copy(down_hbm.at[0], down_ref, down_sem)
    fetch.start()
    copies = []
    for k in range(n_nar):
        to = lax.rem(at_ref[0] + k, n_nar)
        for i in range(2):
            rows = pl.ds(pl.multiple_of((to * 2 + i) * part, 64), part)
            for m, source in enumerate((gate_hbm, up_hbm)):
                place = outs[k].at[i, :, m * units : (m + 1) * units]
                copies.append(pltpu.make_async_copy(source.at[0, rows], place, sems.at[k, i, m]))
    for copy in copies:
        copy.start()
    fetch.wait()
    turned_ref[...] = jnp.transpose(down_ref[...])
    for k in range(n_nar):
        to = lax.rem(at_ref[0] + k, n_nar)
        for i in range(2):
            rows = pl.ds(pl.multiple_of((i * n_nar + to) * part, 64), part)
            outs[k][2, :, i * units : (i + 1) * units] = turned_ref[rows]
    for copy in copies:
        copy.wait()


def arrived_body(*refs):
    refs[-1][...] = jnp.zeros(refs[-1].shape, F32)


def pick_body(part, top, far_ref, rows_ref, out_ref, weight_ref):
    blocks, tok, _ = rows_ref.shape
    count = blocks * tok
    rows = rows_ref[...].reshape(count, LANES)
    extra = rows[:, part : part + 3 * top]
    eye = (
        lax.broadcasted_iota(I32, (3 * top, 3 * top), 0) == lax.broadcasted_iota(I32, (3 * top, 3 * top), 1)
    ).astype(BF16)
    extra = lax.dot_general(eye, extra, (((1,), (1,)), ((), ())), preferred_element_type=F32)
    j = lax.broadcasted_iota(I32, (8, count), 0)
    z_count = 2 * lax.axis_size(FAR)
    expert = (((j // 4) * z_count + far_ref[0] * 2 + (j // 2) % 2) * 2 + j % 2).astype(F32)
    chosen = jnp.zeros((8, count), F32)
    gate = jnp.zeros((8, count), F32)
    for k in range(top):
        same = extra[k : k + 1] == expert
        chosen = jnp.where(same, 1.0, chosen)
        value = extra[top + k : top + k + 1] + extra[2 * top + k : 2 * top + k + 1]
        gate = gate + jnp.where(same, value, 0.0)
    first = lax.broadcasted_iota(I32, (count, count), 0)
    second = lax.broadcasted_iota(I32, (count, count), 1)
    before = ((first < second) & (first // tok == second // tok)).astype(BF16)
    place = jnp.dot(chosen.astype(BF16), before, preferred_element_type=F32)
    block = (lax.broadcasted_iota(I32, (8, count), 1) // tok).astype(F32)
    slot = jnp.where(chosen > 0.0, place + block * CAP, -1.0)
    want = lax.broadcasted_iota(I32, (8, blocks * CAP, count), 1).astype(F32)
    hit = slot[:, None, :] == want
    picker = jnp.where(hit, 1.0, 0.0).astype(BF16).reshape(8 * blocks * CAP, count)
    weight = jnp.where(hit, gate[:, None, :], 0.0).reshape(8 * blocks * CAP, count)
    high = weight.astype(BF16)
    weight_ref[:, :count] = high
    weight_ref[:, count:] = (weight - high.astype(F32)).astype(BF16)
    got = jnp.dot(picker, rows[:, :part], preferred_element_type=F32).astype(BF16)
    got = got.reshape(8, blocks * CAP, part)
    out_ref[:8] = got
    out_ref[8:] = got


def gate_up_body(n_nar, me_ref, rows_ref, *rest):
    parts, out_ref = rest[:n_nar], rest[-1]
    slots, part = out_ref.shape[1], rows_ref.shape[2]
    half = rows_ref.shape[0] // 2
    left = rows_ref[:half].reshape(slots, part)
    right = rows_ref[half:].reshape(slots, part)
    for k in range(n_nar):
        act = jnp.dot(left, parts[k][0], preferred_element_type=F32)
        act = act + jnp.dot(right, parts[k][1], preferred_element_type=F32)
        out_ref[lax.rem(me_ref[0] - k + n_nar, n_nar)] = act.astype(BF16)


def inner_body(acts_ref, out_ref):
    count, _, units = out_ref.shape
    act = sum(acts_ref[i].astype(F32) for i in range(count))
    gate, up = act[:, :units], act[:, units:]
    inner = (gate / (1.0 + jnp.exp(-gate)) * up).astype(BF16)
    for i in range(count):
        out_ref[i] = inner


def down_body(n_nar, me_ref, inner_ref, *rest):
    parts, out_ref = rest[:n_nar], rest[-1]
    half = out_ref.shape[0] // 2
    units = inner_ref.shape[2]
    left = jnp.concatenate([inner_ref[lax.rem(me_ref[0] - k + n_nar, n_nar)] for k in range(n_nar)], axis=1)
    for i in range(2):
        right = jnp.concatenate([parts[k][2, :, i * units : (i + 1) * units] for k in range(n_nar)], axis=1)
        out = lax.dot_general(left, right, (((1,), (1,)), ((), ())), preferred_element_type=F32).astype(BF16)
        out_ref[i * half : (i + 1) * half] = out.reshape(half, -1, out.shape[1])


def combine_body(rows_ref, weight_ref, out_ref):
    blocks, tok, part = out_ref.shape
    half = rows_ref.shape[0] // 2
    weight = weight_ref[...]
    total = 0.0
    for i in range(2):
        rows = rows_ref[i * half : (i + 1) * half].reshape(weight.shape[0], part)
        total = total + lax.dot_general(weight, rows, (((0,), (0,)), ((), ())), preferred_element_type=F32)
    count = blocks * tok
    out_ref[...] = (total[:count] + total[count:]).astype(BF16).reshape(blocks, tok, part)


def per_device(hidden, routes, route_gates, gate_proj, up_proj, down_proj):
    tok, width = hidden.shape
    top = routes.shape[1]
    n_grp, n_nar, n_far = lax.axis_size("grp"), lax.axis_size("narrow"), lax.axis_size(FAR)
    g, n = lax.axis_index("grp"), lax.axis_index("narrow")
    far = lax.axis_index(FAR).astype(I32).reshape(1)
    units = gate_proj.shape[2]
    part = width // (n_grp * n_nar)
    near = 16
    slots = 8 * n_far * CAP

    at = jnp.stack([n, g]).astype(I32)
    rows = call(
        functools.partial(rows_body, part, top),
        jax.ShapeDtypeStruct((n_far, tok, LANES), BF16),
        [SMEM, HBM, HBM, HBM],
        [at, hidden, routes.T, route_gates.T],
        scratch=[
            pltpu.VMEM((tok, LANES), BF16),
            pltpu.VMEM((top, tok), I32),
            pltpu.VMEM((top, tok), F32),
            pltpu.SemaphoreType.DMA((3,)),
        ],
        mib=60,
    )
    rows = exchange(rows, FAR)

    parts = call(
        functools.partial(pack_body, n_nar, part),
        [jax.ShapeDtypeStruct((3, part, 2 * units), BF16)] * n_nar,
        [SMEM, HBM, HBM, HBM],
        [at, gate_proj, up_proj, down_proj],
        scratch=[
            pltpu.VMEM((units, width), BF16),
            pltpu.VMEM((width, units), BF16),
            pltpu.SemaphoreType.DMA((n_nar, 2, 2)),
            pltpu.SemaphoreType.DMA,
        ],
        mib=60,
    )
    parts = list(parts)
    for k in range(1, n_nar):
        parts[k] = lax.ppermute(parts[k], "narrow", [(i, (i + k) % n_nar) for i in range(n_nar)])
    arrived = call(
        arrived_body, jax.ShapeDtypeStruct((8, 128), F32), [ANY] * (n_nar - 1), parts[1:], flops=HOLD
    )

    picked, weight = call(
        functools.partial(pick_body, part, top),
        [
            jax.ShapeDtypeStruct((near, n_far * CAP, part), BF16),
            jax.ShapeDtypeStruct((slots, 2 * n_far * tok), BF16),
        ],
        [SMEM, VMEM],
        [far, rows],
        flops=2 * slots * n_far * tok * part,
    )
    rows = exchange(picked, NEAR)

    acts = call(
        functools.partial(gate_up_body, n_nar),
        jax.ShapeDtypeStruct((n_nar, slots, 2 * units), BF16),
        [SMEM, VMEM] + [VMEM] * n_nar + [ANY],
        [at, rows] + parts + [arrived],
        flops=2 * slots * part * 2 * units * 2 * n_nar,
    )
    acts = exchange(acts, "narrow")
    inner = call(inner_body, jax.ShapeDtypeStruct((n_nar, slots, units), BF16), [VMEM], [acts])
    inner = exchange(inner, "narrow")
    outs = call(
        functools.partial(down_body, n_nar),
        jax.ShapeDtypeStruct((near, n_far * CAP, part), BF16),
        [SMEM, VMEM] + [VMEM] * n_nar,
        [at, inner] + parts,
        flops=2 * slots * units * n_nar * 2 * part,
    )
    outs = exchange(outs, NEAR)
    sums = call(
        combine_body,
        jax.ShapeDtypeStruct((n_far, tok, part), BF16),
        [VMEM, VMEM],
        [outs, weight],
        flops=2 * slots * 2 * 2 * n_far * tok * part,
    )
    sums = exchange(sums, FAR)
    return jnp.sum(sums.astype(F32), axis=0).astype(BF16)


def solution(mesh):
    n_grp, n_wide, n_nar = mesh.devices.shape
    fine = Mesh(mesh.devices.reshape(n_grp, 2, n_wide // 8, 2, 2, n_nar), AXES)
    return jax.shard_map(
        per_device,
        mesh=fine,
        in_specs=(
            P(WIDE, None),
            P(WIDE, None),
            P(WIDE, None),
            P(WIDE, None, ("grp", "narrow")),
            P(WIDE, None, ("grp", "narrow")),
            P(WIDE, ("grp", "narrow"), None),
        ),
        out_specs=P(WIDE, ("grp", "narrow")),
        check_vma=False,
    )
```

```python
import functools

import jax
import jax.numpy as jnp
from jax import lax
from jax.experimental import pallas as pl
from jax.experimental.pallas import tpu as pltpu
from jax.sharding import Mesh, PartitionSpec as P

CAP = 8
F32 = jnp.float32
BF16 = jnp.bfloat16
I32 = jnp.int32
FAR = "zfar"
NEAR = ("grp", "ylo", "znear", "core")
AXES = ("grp", "ylo", "zfar", "znear", "core", "narrow")
WIDE = ("ylo", "zfar", "znear", "core")
LANES = 512
HOLD = 200 * 10**9

VMEM = pl.BlockSpec(memory_space=pltpu.VMEM)
SMEM = pl.BlockSpec(memory_space=pltpu.SMEM)
ANY = pl.BlockSpec(memory_space=pl.ANY)
HBM = pl.BlockSpec(memory_space=pltpu.HBM)


def call(body, outs, specs, args, flops=0, scratch=(), mib=16, place=None):
    single = not isinstance(outs, list)
    outs = [outs] if single else outs
    nbytes = sum(a.size * a.dtype.itemsize for a in args) + sum(o.size * o.dtype.itemsize for o in outs)
    got = pl.pallas_call(
        body,
        out_shape=outs,
        in_specs=specs,
        out_specs=[place or VMEM] * len(outs),
        scratch_shapes=list(scratch),
        compiler_params=pltpu.CompilerParams(vmem_limit_bytes=mib * 1024 * 1024),
        cost_estimate=pl.CostEstimate(flops=flops, bytes_accessed=nbytes, transcendentals=0),
    )(*args)
    return got[0] if single else got


def exchange(x, axis):
    return lax.all_to_all(x, axis, split_axis=0, concat_axis=0, tiled=True)


def rows_body(part, top, hidden_hbm, routes_hbm, gates_hbm, out_ref, wide_ref, routes_ref, gates_ref, sems):
    count, tok, lanes = out_ref.shape
    odd = lax.axis_index("grp")
    start = pl.multiple_of(lax.axis_index("narrow") * 2 * part + odd * (part // 128 * 128), 128)
    copies = [
        pltpu.make_async_copy(hidden_hbm.at[:, pl.ds(start, LANES)], wide_ref, sems.at[0]),
        pltpu.make_async_copy(routes_hbm, routes_ref, sems.at[1]),
        pltpu.make_async_copy(gates_hbm, gates_ref, sems.at[2]),
    ]
    for copy in copies:
        copy.start()
    for copy in copies:
        copy.wait()
    wide = wide_ref[...].astype(F32)
    mine = jnp.where(odd == 1, wide[:, LANES - part :], wide[:, :part])
    gates = gates_ref[...]
    high = gates.astype(BF16).astype(F32)
    extra = jnp.concatenate([routes_ref[...].astype(F32), high, gates - high], axis=0).astype(BF16)
    eye = (lax.broadcasted_iota(I32, (tok, tok), 0) == lax.broadcasted_iota(I32, (tok, tok), 1)).astype(BF16)
    extra = lax.dot_general(eye, extra, (((1,), (1,)), ((), ())), preferred_element_type=F32)
    spare = jnp.zeros((tok, lanes - part - 3 * top), F32)
    rows = jnp.concatenate([mine, extra, spare], axis=1).astype(BF16)
    for i in range(count):
        out_ref[i] = rows


def pack_body(n_nar, part, gate_hbm, up_hbm, down_hbm, *rest):
    outs, (down_ref, turned_ref, sems, turned_sems, down_sem) = rest[:n_nar], rest[n_nar:]
    units = gate_hbm.shape[2]
    me = lax.axis_index("narrow")
    fetch = pltpu.make_async_copy(down_hbm.at[0], down_ref, down_sem)
    fetch.start()
    copies = []
    for k in range(1, n_nar + 1):
        k = k % n_nar
        to = lax.rem(me + k, n_nar)
        for i in range(2):
            rows = pl.ds(pl.multiple_of((to * 2 + i) * part, 64), part)
            for m, source in enumerate((gate_hbm, up_hbm)):
                place = outs[k].at[i, :, m * units : (m + 1) * units]
                copies.append(pltpu.make_async_copy(source.at[0, rows], place, sems.at[k, i, m]))
    for copy in copies:
        copy.start()
    fetch.wait()
    turned_ref[...] = jnp.transpose(down_ref[...])
    for k in range(n_nar):
        to = lax.rem(me + k, n_nar)
        for i in range(2):
            rows = pl.ds(pl.multiple_of((i * n_nar + to) * part, 64), part)
            place = outs[k].at[2, :, i * units : (i + 1) * units]
            copy = pltpu.make_async_copy(turned_ref.at[rows], place, turned_sems.at[k, i])
            copy.start()
            copies.append(copy)
    for copy in copies:
        copy.wait()


def arrived_body(*refs):
    refs[-1][...] = jnp.zeros(refs[-1].shape, F32)


def slots_of(part, top, rows_ref):
    blocks, tok, _ = rows_ref.shape
    count = blocks * tok
    extra = rows_ref[...].reshape(count, LANES)[:, part : part + 3 * top]
    eye = (
        lax.broadcasted_iota(I32, (3 * top, 3 * top), 0) == lax.broadcasted_iota(I32, (3 * top, 3 * top), 1)
    ).astype(BF16)
    extra = lax.dot_general(eye, extra, (((1,), (1,)), ((), ())), preferred_element_type=F32)
    j = lax.broadcasted_iota(I32, (8, count), 0)
    z_count = 2 * lax.axis_size(FAR)
    expert = (((j // 4) * z_count + lax.axis_index(FAR) * 2 + (j // 2) % 2) * 2 + j % 2).astype(F32)
    chosen = jnp.zeros((8, count), F32)
    gate = jnp.zeros((8, count), F32)
    for k in range(top):
        same = extra[k : k + 1] == expert
        chosen = jnp.where(same, 1.0, chosen)
        value = extra[top + k : top + k + 1] + extra[2 * top + k : 2 * top + k + 1]
        gate = gate + jnp.where(same, value, 0.0)
    first = lax.broadcasted_iota(I32, (count, count), 0)
    second = lax.broadcasted_iota(I32, (count, count), 1)
    before = ((first < second) & (first // tok == second // tok)).astype(BF16)
    place = jnp.dot(chosen.astype(BF16), before, preferred_element_type=F32)
    block = (lax.broadcasted_iota(I32, (8, count), 1) // tok).astype(F32)
    slot = jnp.where(chosen > 0.0, place + block * CAP, -1.0)
    want = lax.broadcasted_iota(I32, (8, blocks * CAP, count), 1).astype(F32)
    return slot[:, None, :] == want, gate


def pick_body(part, top, rows_ref, out_ref):
    near, half, _ = out_ref.shape
    near = near // 2
    hit, _ = slots_of(part, top, rows_ref)
    picker = jnp.where(hit, 1.0, 0.0).astype(BF16)
    rows = rows_ref[...].reshape(-1, LANES)[:, :part]
    sides = []
    for i in range(2):
        left = picker[:, i * half : (i + 1) * half].reshape(near * half, -1)
        sides.append(jnp.dot(left, rows, preferred_element_type=F32))
    got = jnp.concatenate(sides, axis=1).astype(BF16).reshape(near, half, 2 * part)
    out_ref[:near] = got
    out_ref[near:] = got


def weight_body(part, top, rows_ref, out_ref):
    _, half, count = out_ref.shape
    hit, gate = slots_of(part, top, rows_ref)
    weight = jnp.where(hit, gate[:, None, :], 0.0)
    high = weight.astype(BF16)
    low = (weight - high.astype(F32)).astype(BF16)
    both = jnp.concatenate([high, low], axis=2)
    near = both.shape[0]
    for i in range(2):
        side = both[:, i * (both.shape[1] // 2) : (i + 1) * (both.shape[1] // 2)]
        out_ref[i] = side.reshape(half, count)


def two_sides(rows, part):
    rows = rows.reshape(-1, 2 * part)
    return jnp.concatenate([rows[:, :part], rows[:, part:]], axis=0)


def gate_up_body(n_nar, rows_ref, *rest):
    parts, out_ref = rest[:n_nar], rest[-1]
    me = lax.axis_index("narrow")
    part = rows_ref.shape[2] // 2
    half = rows_ref.shape[0] // 2
    left = two_sides(rows_ref[:half], part)
    right = two_sides(rows_ref[half:], part)
    for k in range(n_nar):
        act = jnp.dot(left, parts[k][0], preferred_element_type=F32)
        act = act + jnp.dot(right, parts[k][1], preferred_element_type=F32)
        out_ref[lax.rem(me - k + n_nar, n_nar)] = act.astype(BF16)


def inner_body(acts_ref, out_ref):
    count, _, units = out_ref.shape
    act = sum(acts_ref[i].astype(F32) for i in range(count))
    gate, up = act[:, :units], act[:, units:]
    inner = (gate / (1.0 + jnp.exp(-gate)) * up).astype(BF16)
    for i in range(count):
        out_ref[i] = inner


def down_body(n_nar, inner_ref, *rest):
    parts, out_ref = rest[:n_nar], rest[-1]
    me = lax.axis_index("narrow")
    near = out_ref.shape[0] // 2
    units = inner_ref.shape[2]
    left = jnp.concatenate([inner_ref[lax.rem(me - k + n_nar, n_nar)] for k in range(n_nar)], axis=1)
    count = left.shape[0] // 2
    for i in range(2):
        right = jnp.concatenate([parts[k][2, :, i * units : (i + 1) * units] for k in range(n_nar)], axis=1)
        out = lax.dot_general(left, right, (((1,), (1,)), ((), ())), preferred_element_type=F32)
        out = jnp.concatenate([out[:count], out[count:]], axis=1).astype(BF16)
        out_ref[i * near : (i + 1) * near] = out.reshape(near, -1, out.shape[1])


def combine_body(rows_ref, weight_ref, out_ref):
    blocks, half, width = out_ref.shape
    near = rows_ref.shape[0] // 2
    part = width // 2
    total = 0.0
    for i in range(2):
        rows = rows_ref[i * near : (i + 1) * near].reshape(-1, width)
        for h in range(2):
            side = rows[:, h * part : (h + 1) * part]
            total = total + lax.dot_general(
                weight_ref[h], side, (((0,), (0,)), ((), ())), preferred_element_type=F32
            )
    count = total.shape[0] // 2
    total = (total[:count] + total[count:]).reshape(blocks, 2 * half, part)
    total = jnp.concatenate([total[:, :half], total[:, half:]], axis=2)
    out_ref[...] = total.astype(BF16)


def last_body(sums_ref, out_ref):
    total = sum(sums_ref[i].astype(F32) for i in range(sums_ref.shape[0]))
    half, width = total.shape
    out_ref[:half] = total[:, : width // 2].astype(BF16)
    out_ref[half:] = total[:, width // 2 :].astype(BF16)


def per_device(hidden, routes, route_gates, gate_proj, up_proj, down_proj):
    tok, width = hidden.shape
    top = routes.shape[1]
    n_grp, n_nar, n_far = lax.axis_size("grp"), lax.axis_size("narrow"), lax.axis_size(FAR)
    units = gate_proj.shape[2]
    part = width // (n_grp * n_nar)
    near = 16
    slots = 8 * n_far * CAP

    rows = call(
        functools.partial(rows_body, part, top),
        jax.ShapeDtypeStruct((n_far, tok, LANES), BF16),
        [HBM, HBM, HBM],
        [hidden, routes.T, route_gates.T],
        scratch=[
            pltpu.VMEM((tok, LANES), BF16),
            pltpu.VMEM((top, tok), I32),
            pltpu.VMEM((top, tok), F32),
            pltpu.SemaphoreType.DMA((3,)),
        ],
        mib=60,
    )
    rows = exchange(rows, FAR)

    parts = call(
        functools.partial(pack_body, n_nar, part),
        [jax.ShapeDtypeStruct((3, part, 2 * units), BF16)] * n_nar,
        [HBM, HBM, HBM],
        [gate_proj, up_proj, down_proj],
        place=HBM,
        scratch=[
            pltpu.VMEM((units, width), BF16),
            pltpu.VMEM((width, units), BF16),
            pltpu.SemaphoreType.DMA((n_nar, 2, 2)),
            pltpu.SemaphoreType.DMA((n_nar, 2)),
            pltpu.SemaphoreType.DMA,
        ],
        mib=60,
    )
    parts = list(parts)
    for k in range(1, n_nar):
        parts[k] = lax.ppermute(parts[k], "narrow", [(i, (i + k) % n_nar) for i in range(n_nar)])
    arrived = call(
        arrived_body, jax.ShapeDtypeStruct((8, 128), F32), [ANY] * (n_nar - 1), parts[1:], flops=HOLD
    )

    half = n_far * CAP // 2
    picked = call(
        functools.partial(pick_body, part, top),
        jax.ShapeDtypeStruct((near, half, 2 * part), BF16),
        [VMEM],
        [rows],
        flops=2 * slots * n_far * tok * part,
    )
    weight = call(
        functools.partial(weight_body, part, top),
        jax.ShapeDtypeStruct((2, slots // 2, 2 * n_far * tok), BF16),
        [VMEM],
        [rows],
    )
    rows = exchange(picked, NEAR)

    acts = call(
        functools.partial(gate_up_body, n_nar),
        jax.ShapeDtypeStruct((n_nar, slots, 2 * units), BF16),
        [VMEM] + [VMEM] * n_nar + [ANY],
        [rows] + parts + [arrived],
        flops=2 * slots * part * 2 * units * 2 * n_nar,
    )
    acts = exchange(acts, "narrow")
    inner = call(inner_body, jax.ShapeDtypeStruct((n_nar, slots, units), BF16), [VMEM], [acts])
    inner = exchange(inner, "narrow")
    outs = call(
        functools.partial(down_body, n_nar),
        jax.ShapeDtypeStruct((near, half, 2 * part), BF16),
        [VMEM] + [VMEM] * n_nar,
        [inner] + parts,
        flops=2 * slots * units * n_nar * 2 * part,
    )
    outs = exchange(outs, NEAR)
    sums = call(
        combine_body,
        jax.ShapeDtypeStruct((n_far, tok // 2, 2 * part), BF16),
        [VMEM, VMEM],
        [outs, weight],
        flops=2 * slots * 2 * 2 * n_far * tok * part,
    )
    sums = exchange(sums, FAR)
    return call(last_body, jax.ShapeDtypeStruct((tok, part), BF16), [VMEM], [sums])


def solution(mesh):
    n_grp, n_wide, n_nar = mesh.devices.shape
    fine = Mesh(mesh.devices.reshape(n_grp, 2, n_wide // 8, 2, 2, n_nar), AXES)
    return jax.shard_map(
        per_device,
        mesh=fine,
        in_specs=(
            P(WIDE, None),
            P(WIDE, None),
            P(WIDE, None),
            P(WIDE, None, ("grp", "narrow")),
            P(WIDE, None, ("grp", "narrow")),
            P(WIDE, ("grp", "narrow"), None),
        ),
        out_specs=P(WIDE, ("grp", "narrow")),
        check_vma=False,
    )
```

```python
import functools

import jax
import jax.numpy as jnp
from jax import lax
from jax.experimental import pallas as pl
from jax.experimental.pallas import tpu as pltpu
from jax.sharding import Mesh, PartitionSpec as P

CAP = 8
F32 = jnp.float32
BF16 = jnp.bfloat16
I32 = jnp.int32
FAR = "zfar"
NEAR = ("grp", "ylo", "znear", "core")
AXES = ("grp", "ylo", "zfar", "znear", "core", "narrow")
WIDE = ("ylo", "zfar", "znear", "core")
LANES = 512
HOLD = 200 * 10**9

VMEM = pl.BlockSpec(memory_space=pltpu.VMEM)
SMEM = pl.BlockSpec(memory_space=pltpu.SMEM)
ANY = pl.BlockSpec(memory_space=pl.ANY)
HBM = pl.BlockSpec(memory_space=pltpu.HBM)


def call(body, outs, specs, args, flops=0, scratch=(), mib=16):
    single = not isinstance(outs, list)
    outs = [outs] if single else outs
    nbytes = sum(a.size * a.dtype.itemsize for a in args) + sum(o.size * o.dtype.itemsize for o in outs)
    got = pl.pallas_call(
        body,
        out_shape=outs,
        in_specs=specs,
        out_specs=[VMEM] * len(outs),
        scratch_shapes=list(scratch),
        compiler_params=pltpu.CompilerParams(vmem_limit_bytes=mib * 1024 * 1024),
        cost_estimate=pl.CostEstimate(flops=flops, bytes_accessed=nbytes, transcendentals=0),
    )(*args)
    return got[0] if single else got


def exchange(x, axis):
    return lax.all_to_all(x, axis, split_axis=0, concat_axis=0, tiled=True)


def rows_body(part, top, hidden_hbm, routes_hbm, gates_hbm, out_ref, wide_ref, routes_ref, gates_ref, sems):
    count, tok, lanes = out_ref.shape
    odd = lax.axis_index("grp")
    start = pl.multiple_of(lax.axis_index("narrow") * 2 * part + odd * (part // 128 * 128), 128)
    copies = [
        pltpu.make_async_copy(hidden_hbm.at[:, pl.ds(start, LANES)], wide_ref, sems.at[0]),
        pltpu.make_async_copy(routes_hbm, routes_ref, sems.at[1]),
        pltpu.make_async_copy(gates_hbm, gates_ref, sems.at[2]),
    ]
    for copy in copies:
        copy.start()
    for copy in copies:
        copy.wait()
    wide = wide_ref[...].astype(F32)
    mine = jnp.where(odd == 1, wide[:, LANES - part :], wide[:, :part])
    gates = gates_ref[...]
    high = gates.astype(BF16).astype(F32)
    extra = jnp.concatenate([routes_ref[...].astype(F32), high, gates - high], axis=0).astype(BF16)
    eye = (lax.broadcasted_iota(I32, (tok, tok), 0) == lax.broadcasted_iota(I32, (tok, tok), 1)).astype(BF16)
    extra = lax.dot_general(eye, extra, (((1,), (1,)), ((), ())), preferred_element_type=F32)
    spare = jnp.zeros((tok, lanes - part - 3 * top), F32)
    rows = jnp.concatenate([mine, extra, spare], axis=1).astype(BF16)
    for i in range(count):
        out_ref[i] = rows


def pack_body(n_nar, part, gate_hbm, up_hbm, down_hbm, *rest):
    outs, (down_ref, turned_ref, sems, down_sem) = rest[:n_nar], rest[n_nar:]
    units = gate_hbm.shape[2]
    me = lax.axis_index("narrow")
    fetch = pltpu.make_async_copy(down_hbm.at[0], down_ref, down_sem)
    fetch.start()
    copies = []
    for k in range(n_nar):
        to = lax.rem(me + k, n_nar)
        for i in range(2):
            rows = pl.ds(pl.multiple_of((to * 2 + i) * part, 64), part)
            for m, source in enumerate((gate_hbm, up_hbm)):
                place = outs[k].at[i, :, m * units : (m + 1) * units]
                copies.append(pltpu.make_async_copy(source.at[0, rows], place, sems.at[k, i, m]))
    for copy in copies:
        copy.start()
    fetch.wait()
    turned_ref[...] = jnp.transpose(down_ref[...])
    for k in range(n_nar):
        to = lax.rem(me + k, n_nar)
        for i in range(2):
            rows = pl.ds(pl.multiple_of((i * n_nar + to) * part, 64), part)
            outs[k][2, :, i * units : (i + 1) * units] = turned_ref[rows]
    for copy in copies:
        copy.wait()


def arrived_body(*refs):
    refs[-1][...] = jnp.zeros(refs[-1].shape, F32)


def slots_of(part, top, rows_ref):
    blocks, tok, _ = rows_ref.shape
    count = blocks * tok
    extra = rows_ref[...].reshape(count, LANES)[:, part : part + 3 * top]
    eye = (
        lax.broadcasted_iota(I32, (3 * top, 3 * top), 0) == lax.broadcasted_iota(I32, (3 * top, 3 * top), 1)
    ).astype(BF16)
    extra = lax.dot_general(eye, extra, (((1,), (1,)), ((), ())), preferred_element_type=F32)
    j = lax.broadcasted_iota(I32, (8, count), 0)
    z_count = 2 * lax.axis_size(FAR)
    expert = (((j // 4) * z_count + lax.axis_index(FAR) * 2 + (j // 2) % 2) * 2 + j % 2).astype(F32)
    chosen = jnp.zeros((8, count), F32)
    gate = jnp.zeros((8, count), F32)
    for k in range(top):
        same = extra[k : k + 1] == expert
        chosen = jnp.where(same, 1.0, chosen)
        value = extra[top + k : top + k + 1] + extra[2 * top + k : 2 * top + k + 1]
        gate = gate + jnp.where(same, value, 0.0)
    first = lax.broadcasted_iota(I32, (count, count), 0)
    second = lax.broadcasted_iota(I32, (count, count), 1)
    before = ((first < second) & (first // tok == second // tok)).astype(BF16)
    place = jnp.dot(chosen.astype(BF16), before, preferred_element_type=F32)
    block = (lax.broadcasted_iota(I32, (8, count), 1) // tok).astype(F32)
    slot = jnp.where(chosen > 0.0, place + block * CAP, -1.0)
    want = lax.broadcasted_iota(I32, (8, blocks * CAP, count), 1).astype(F32)
    return slot[:, None, :] == want, gate


def pick_body(part, top, rows_ref, out_ref):
    near, half, _ = out_ref.shape
    near = near // 2
    hit, _ = slots_of(part, top, rows_ref)
    picker = jnp.where(hit, 1.0, 0.0).astype(BF16)
    rows = rows_ref[...].reshape(-1, LANES)[:, :part]
    sides = []
    for i in range(2):
        left = picker[:, i * half : (i + 1) * half].reshape(near * half, -1)
        sides.append(jnp.dot(left, rows, preferred_element_type=F32))
    got = jnp.concatenate(sides, axis=1).astype(BF16).reshape(near, half, 2 * part)
    out_ref[:near] = got
    out_ref[near:] = got


def weight_body(part, top, rows_ref, out_ref):
    _, half, count = out_ref.shape
    hit, gate = slots_of(part, top, rows_ref)
    weight = jnp.where(hit, gate[:, None, :], 0.0)
    high = weight.astype(BF16)
    low = (weight - high.astype(F32)).astype(BF16)
    both = jnp.concatenate([high, low], axis=2)
    near = both.shape[0]
    for i in range(2):
        side = both[:, i * (both.shape[1] // 2) : (i + 1) * (both.shape[1] // 2)]
        out_ref[i] = side.reshape(half, count)


def two_sides(rows, part):
    rows = rows.reshape(-1, 2 * part)
    return jnp.concatenate([rows[:, :part], rows[:, part:]], axis=0)


def gate_up_body(n_nar, rows_ref, *rest):
    parts, out_ref = rest[:n_nar], rest[-1]
    me = lax.axis_index("narrow")
    part = rows_ref.shape[2] // 2
    half = rows_ref.shape[0] // 2
    left = two_sides(rows_ref[:half], part)
    right = two_sides(rows_ref[half:], part)
    for k in range(n_nar):
        act = jnp.dot(left, parts[k][0], preferred_element_type=F32)
        act = act + jnp.dot(right, parts[k][1], preferred_element_type=F32)
        out_ref[lax.rem(me - k + n_nar, n_nar)] = act.astype(BF16)


def inner_body(acts_ref, out_ref):
    count, _, units = out_ref.shape
    act = sum(acts_ref[i].astype(F32) for i in range(count))
    gate, up = act[:, :units], act[:, units:]
    inner = (gate / (1.0 + jnp.exp(-gate)) * up).astype(BF16)
    for i in range(count):
        out_ref[i] = inner


def down_body(n_nar, inner_ref, *rest):
    parts, out_ref = rest[:n_nar], rest[-1]
    me = lax.axis_index("narrow")
    near = out_ref.shape[0] // 2
    units = inner_ref.shape[2]
    left = jnp.concatenate([inner_ref[lax.rem(me - k + n_nar, n_nar)] for k in range(n_nar)], axis=1)
    count = left.shape[0] // 2
    for i in range(2):
        right = jnp.concatenate([parts[k][2, :, i * units : (i + 1) * units] for k in range(n_nar)], axis=1)
        out = lax.dot_general(left, right, (((1,), (1,)), ((), ())), preferred_element_type=F32)
        out = jnp.concatenate([out[:count], out[count:]], axis=1).astype(BF16)
        out_ref[i * near : (i + 1) * near] = out.reshape(near, -1, out.shape[1])


def combine_body(rows_ref, weight_ref, out_ref):
    blocks, half, width = out_ref.shape
    near = rows_ref.shape[0] // 2
    part = width // 2
    total = 0.0
    for i in range(2):
        rows = rows_ref[i * near : (i + 1) * near].reshape(-1, width)
        for h in range(2):
            side = rows[:, h * part : (h + 1) * part]
            total = total + lax.dot_general(
                weight_ref[h], side, (((0,), (0,)), ((), ())), preferred_element_type=F32
            )
    count = total.shape[0] // 2
    total = (total[:count] + total[count:]).reshape(blocks, 2 * half, part)
    total = jnp.concatenate([total[:, :half], total[:, half:]], axis=2)
    out_ref[...] = total.astype(BF16)


def last_body(sums_ref, out_ref):
    total = sum(sums_ref[i].astype(F32) for i in range(sums_ref.shape[0]))
    half, width = total.shape
    out_ref[:half] = total[:, : width // 2].astype(BF16)
    out_ref[half:] = total[:, width // 2 :].astype(BF16)


def per_device(hidden, routes, route_gates, gate_proj, up_proj, down_proj):
    tok, width = hidden.shape
    top = routes.shape[1]
    n_grp, n_nar, n_far = lax.axis_size("grp"), lax.axis_size("narrow"), lax.axis_size(FAR)
    units = gate_proj.shape[2]
    part = width // (n_grp * n_nar)
    near = 16
    slots = 8 * n_far * CAP

    rows = call(
        functools.partial(rows_body, part, top),
        jax.ShapeDtypeStruct((n_far, tok, LANES), BF16),
        [HBM, HBM, HBM],
        [hidden, routes.T, route_gates.T],
        scratch=[
            pltpu.VMEM((tok, LANES), BF16),
            pltpu.VMEM((top, tok), I32),
            pltpu.VMEM((top, tok), F32),
            pltpu.SemaphoreType.DMA((3,)),
        ],
        mib=60,
    )
    rows = exchange(rows, FAR)

    parts = call(
        functools.partial(pack_body, n_nar, part),
        [jax.ShapeDtypeStruct((3, part, 2 * units), BF16)] * n_nar,
        [HBM, HBM, HBM],
        [gate_proj, up_proj, down_proj],
        scratch=[
            pltpu.VMEM((units, width), BF16),
            pltpu.VMEM((width, units), BF16),
            pltpu.SemaphoreType.DMA((n_nar, 2, 2)),
            pltpu.SemaphoreType.DMA,
        ],
        mib=60,
    )
    parts = list(parts)
    for k in range(1, n_nar):
        parts[k] = lax.ppermute(parts[k], "narrow", [(i, (i + k) % n_nar) for i in range(n_nar)])
    arrived = call(
        arrived_body, jax.ShapeDtypeStruct((8, 128), F32), [ANY] * (n_nar - 1), parts[1:], flops=HOLD
    )

    half = n_far * CAP // 2
    picked = call(
        functools.partial(pick_body, part, top),
        jax.ShapeDtypeStruct((near, half, 2 * part), BF16),
        [VMEM],
        [rows],
        flops=2 * slots * n_far * tok * part,
    )
    weight = call(
        functools.partial(weight_body, part, top),
        jax.ShapeDtypeStruct((2, slots // 2, 2 * n_far * tok), BF16),
        [VMEM],
        [rows],
    )
    rows = exchange(picked, NEAR)

    acts = call(
        functools.partial(gate_up_body, n_nar),
        jax.ShapeDtypeStruct((n_nar, slots, 2 * units), BF16),
        [VMEM] + [VMEM] * n_nar + [ANY],
        [rows] + parts + [arrived],
        flops=2 * slots * part * 2 * units * 2 * n_nar,
    )
    acts = exchange(acts, "narrow")
    inner = call(inner_body, jax.ShapeDtypeStruct((n_nar, slots, units), BF16), [VMEM], [acts])
    inner = exchange(inner, "narrow")
    outs = call(
        functools.partial(down_body, n_nar),
        jax.ShapeDtypeStruct((near, half, 2 * part), BF16),
        [VMEM] + [VMEM] * n_nar,
        [inner] + parts,
        flops=2 * slots * units * n_nar * 2 * part,
    )
    outs = exchange(outs, NEAR)
    sums = call(
        combine_body,
        jax.ShapeDtypeStruct((n_far, tok // 2, 2 * part), BF16),
        [VMEM, VMEM],
        [outs, weight],
        flops=2 * slots * 2 * 2 * n_far * tok * part,
    )
    sums = exchange(sums, FAR)
    return call(last_body, jax.ShapeDtypeStruct((tok, part), BF16), [VMEM], [sums])


def solution(mesh):
    n_grp, n_wide, n_nar = mesh.devices.shape
    fine = Mesh(mesh.devices.reshape(n_grp, 2, n_wide // 8, 2, 2, n_nar), AXES)
    return jax.shard_map(
        per_device,
        mesh=fine,
        in_specs=(
            P(WIDE, None),
            P(WIDE, None),
            P(WIDE, None),
            P(WIDE, None, ("grp", "narrow")),
            P(WIDE, None, ("grp", "narrow")),
            P(WIDE, ("grp", "narrow"), None),
        ),
        out_specs=P(WIDE, ("grp", "narrow")),
        check_vma=False,
    )
```

```python
import functools

import jax
import jax.numpy as jnp
from jax import lax
from jax.experimental import pallas as pl
from jax.experimental.pallas import tpu as pltpu
from jax.sharding import Mesh, PartitionSpec as P

CAP = 8
F32 = jnp.float32
BF16 = jnp.bfloat16
I32 = jnp.int32
FAR = "zfar"
NEAR = ("grp", "core", "znear", "ylo")
AXES = ("grp", "ylo", "zfar", "znear", "core", "narrow")
WIDE = ("ylo", "zfar", "znear", "core")
LANES = 512
HOLD = 200 * 10**9

VMEM = pl.BlockSpec(memory_space=pltpu.VMEM)
SMEM = pl.BlockSpec(memory_space=pltpu.SMEM)
ANY = pl.BlockSpec(memory_space=pl.ANY)
HBM = pl.BlockSpec(memory_space=pltpu.HBM)


def call(body, outs, specs, args, flops=0, scratch=(), mib=16):
    single = not isinstance(outs, list)
    outs = [outs] if single else outs
    nbytes = sum(a.size * a.dtype.itemsize for a in args) + sum(o.size * o.dtype.itemsize for o in outs)
    got = pl.pallas_call(
        body,
        out_shape=outs,
        in_specs=specs,
        out_specs=[VMEM] * len(outs),
        scratch_shapes=list(scratch),
        compiler_params=pltpu.CompilerParams(vmem_limit_bytes=mib * 1024 * 1024),
        cost_estimate=pl.CostEstimate(flops=flops, bytes_accessed=nbytes, transcendentals=0),
    )(*args)
    return got[0] if single else got


def exchange(x, axis):
    groups = None
    if isinstance(axis, str):
        count = lax.axis_size(axis)
        groups = [[-i % count for i in range(count)]]
    return lax.all_to_all(x, axis, split_axis=0, concat_axis=0, tiled=True, axis_index_groups=groups)


def rows_body(part, top, hidden_hbm, routes_hbm, gates_hbm, out_ref, wide_ref, routes_ref, gates_ref, sems):
    count, tok, lanes = out_ref.shape
    odd = lax.axis_index("grp")
    start = pl.multiple_of(lax.axis_index("narrow") * 2 * part + odd * (part // 128 * 128), 128)
    copies = [
        pltpu.make_async_copy(hidden_hbm.at[:, pl.ds(start, LANES)], wide_ref, sems.at[0]),
        pltpu.make_async_copy(routes_hbm, routes_ref, sems.at[1]),
        pltpu.make_async_copy(gates_hbm, gates_ref, sems.at[2]),
    ]
    for copy in copies:
        copy.start()
    for copy in copies:
        copy.wait()
    wide = wide_ref[...].astype(F32)
    mine = jnp.where(odd == 1, wide[:, LANES - part :], wide[:, :part])
    gates = gates_ref[...]
    high = gates.astype(BF16).astype(F32)
    extra = jnp.concatenate([routes_ref[...].astype(F32), high, gates - high], axis=0).astype(BF16)
    eye = (lax.broadcasted_iota(I32, (tok, tok), 0) == lax.broadcasted_iota(I32, (tok, tok), 1)).astype(BF16)
    extra = lax.dot_general(eye, extra, (((1,), (1,)), ((), ())), preferred_element_type=F32)
    spare = jnp.zeros((tok, lanes - part - 3 * top), F32)
    rows = jnp.concatenate([mine, extra, spare], axis=1).astype(BF16)
    for i in range(count):
        out_ref[i] = rows


def pack_body(n_nar, part, gate_hbm, up_hbm, down_hbm, *rest):
    outs, (down_ref, turned_ref, sems, down_sem) = rest[:n_nar], rest[n_nar:]
    units = gate_hbm.shape[2]
    me = lax.axis_index("narrow")
    fetch = pltpu.make_async_copy(down_hbm.at[0], down_ref, down_sem)
    fetch.start()
    copies = []
    for k in range(n_nar):
        to = lax.rem(me + k, n_nar)
        for i in range(2):
            rows = pl.ds(pl.multiple_of((to * 2 + i) * part, 64), part)
            for m, source in enumerate((gate_hbm, up_hbm)):
                place = outs[k].at[i, :, m * units : (m + 1) * units]
                copies.append(pltpu.make_async_copy(source.at[0, rows], place, sems.at[k, i, m]))
    for copy in copies:
        copy.start()
    fetch.wait()
    turned_ref[...] = jnp.transpose(down_ref[...])
    for k in range(n_nar):
        to = lax.rem(me + k, n_nar)
        for i in range(2):
            rows = pl.ds(pl.multiple_of((i * n_nar + to) * part, 64), part)
            outs[k][2, :, i * units : (i + 1) * units] = turned_ref[rows]
    for copy in copies:
        copy.wait()


def arrived_body(*refs):
    refs[-1][...] = jnp.zeros(refs[-1].shape, F32)


def slots_of(part, top, rows_ref):
    blocks, tok, _ = rows_ref.shape
    count = blocks * tok
    extra = rows_ref[...].reshape(count, LANES)[:, part : part + 3 * top]
    eye = (
        lax.broadcasted_iota(I32, (3 * top, 3 * top), 0) == lax.broadcasted_iota(I32, (3 * top, 3 * top), 1)
    ).astype(BF16)
    extra = lax.dot_general(eye, extra, (((1,), (1,)), ((), ())), preferred_element_type=F32)
    j = lax.broadcasted_iota(I32, (8, count), 0)
    z_count = 2 * lax.axis_size(FAR)
    expert = (((j % 2) * z_count + lax.axis_index(FAR) * 2 + (j // 2) % 2) * 2 + j // 4).astype(F32)
    chosen = jnp.zeros((8, count), F32)
    gate = jnp.zeros((8, count), F32)
    for k in range(top):
        same = extra[k : k + 1] == expert
        chosen = jnp.where(same, 1.0, chosen)
        value = extra[top + k : top + k + 1] + extra[2 * top + k : 2 * top + k + 1]
        gate = gate + jnp.where(same, value, 0.0)
    first = lax.broadcasted_iota(I32, (count, count), 0)
    second = lax.broadcasted_iota(I32, (count, count), 1)
    before = ((first < second) & (first // tok == second // tok)).astype(BF16)
    place = jnp.dot(chosen.astype(BF16), before, preferred_element_type=F32)
    block = (lax.broadcasted_iota(I32, (8, count), 1) // tok).astype(F32)
    slot = jnp.where(chosen > 0.0, place + block * CAP, -1.0)
    want = lax.broadcasted_iota(I32, (8, blocks * CAP, count), 1).astype(F32)
    return slot[:, None, :] == want, gate


def pick_body(part, top, rows_ref, out_ref):
    near, half, _ = out_ref.shape
    near = near // 2
    hit, _ = slots_of(part, top, rows_ref)
    picker = jnp.where(hit, 1.0, 0.0).astype(BF16)
    rows = rows_ref[...].reshape(-1, LANES)[:, :part]
    sides = []
    for i in range(2):
        left = picker[:, i * half : (i + 1) * half].reshape(near * half, -1)
        sides.append(jnp.dot(left, rows, preferred_element_type=F32))
    got = jnp.concatenate(sides, axis=1).astype(BF16).reshape(near, half, 2 * part)
    out_ref[:near] = got
    out_ref[near:] = got


def weight_body(part, top, rows_ref, out_ref):
    _, half, count = out_ref.shape
    hit, gate = slots_of(part, top, rows_ref)
    weight = jnp.where(hit, gate[:, None, :], 0.0)
    high = weight.astype(BF16)
    low = (weight - high.astype(F32)).astype(BF16)
    both = jnp.concatenate([high, low], axis=2)
    near = both.shape[0]
    for i in range(2):
        side = both[:, i * (both.shape[1] // 2) : (i + 1) * (both.shape[1] // 2)]
        out_ref[i] = side.reshape(half, count)


def two_sides(rows, part):
    rows = rows.reshape(-1, 2 * part)
    return jnp.concatenate([rows[:, :part], rows[:, part:]], axis=0)


def gate_up_body(n_nar, rows_ref, *rest):
    parts, out_ref = rest[:n_nar], rest[-1]
    me = lax.axis_index("narrow")
    part = rows_ref.shape[2] // 2
    half = rows_ref.shape[0] // 2
    left = two_sides(rows_ref[:half], part)
    right = two_sides(rows_ref[half:], part)
    for k in range(n_nar):
        act = jnp.dot(left, parts[k][0], preferred_element_type=F32)
        act = act + jnp.dot(right, parts[k][1], preferred_element_type=F32)
        out_ref[lax.rem(k - me + n_nar, n_nar)] = act.astype(BF16)


def inner_body(acts_ref, out_ref):
    count, _, units = out_ref.shape
    act = sum(acts_ref[i].astype(F32) for i in range(count))
    gate, up = act[:, :units], act[:, units:]
    inner = (gate / (1.0 + jnp.exp(-gate)) * up).astype(BF16)
    for i in range(count):
        out_ref[i] = inner


def down_body(n_nar, inner_ref, *rest):
    parts, out_ref = rest[:n_nar], rest[-1]
    me = lax.axis_index("narrow")
    near = out_ref.shape[0] // 2
    units = inner_ref.shape[2]
    left = jnp.concatenate([inner_ref[lax.rem(k - me + n_nar, n_nar)] for k in range(n_nar)], axis=1)
    count = left.shape[0] // 2
    for i in range(2):
        right = jnp.concatenate([parts[k][2, :, i * units : (i + 1) * units] for k in range(n_nar)], axis=1)
        out = lax.dot_general(left, right, (((1,), (1,)), ((), ())), preferred_element_type=F32)
        out = jnp.concatenate([out[:count], out[count:]], axis=1).astype(BF16)
        out_ref[i * near : (i + 1) * near] = out.reshape(near, -1, out.shape[1])


def combine_body(rows_ref, weight_ref, out_ref):
    blocks, half, width = out_ref.shape
    near = rows_ref.shape[0] // 2
    part = width // 2
    total = 0.0
    for i in range(2):
        rows = rows_ref[i * near : (i + 1) * near].reshape(-1, width)
        for h in range(2):
            side = rows[:, h * part : (h + 1) * part]
            total = total + lax.dot_general(
                weight_ref[h], side, (((0,), (0,)), ((), ())), preferred_element_type=F32
            )
    count = total.shape[0] // 2
    total = (total[:count] + total[count:]).reshape(blocks, 2 * half, part)
    total = jnp.concatenate([total[:, :half], total[:, half:]], axis=2)
    out_ref[...] = total.astype(BF16)


def last_body(sums_ref, out_ref):
    total = sum(sums_ref[i].astype(F32) for i in range(sums_ref.shape[0]))
    half, width = total.shape
    out_ref[:half] = total[:, : width // 2].astype(BF16)
    out_ref[half:] = total[:, width // 2 :].astype(BF16)


def per_device(hidden, routes, route_gates, gate_proj, up_proj, down_proj):
    tok, width = hidden.shape
    top = routes.shape[1]
    n_grp, n_nar, n_far = lax.axis_size("grp"), lax.axis_size("narrow"), lax.axis_size(FAR)
    units = gate_proj.shape[2]
    part = width // (n_grp * n_nar)
    near = 16
    slots = 8 * n_far * CAP

    rows = call(
        functools.partial(rows_body, part, top),
        jax.ShapeDtypeStruct((n_far, tok, LANES), BF16),
        [HBM, HBM, HBM],
        [hidden, routes.T, route_gates.T],
        scratch=[
            pltpu.VMEM((tok, LANES), BF16),
            pltpu.VMEM((top, tok), I32),
            pltpu.VMEM((top, tok), F32),
            pltpu.SemaphoreType.DMA((3,)),
        ],
        mib=60,
    )
    rows = exchange(rows, FAR)

    parts = call(
        functools.partial(pack_body, n_nar, part),
        [jax.ShapeDtypeStruct((3, part, 2 * units), BF16)] * n_nar,
        [HBM, HBM, HBM],
        [gate_proj, up_proj, down_proj],
        scratch=[
            pltpu.VMEM((units, width), BF16),
            pltpu.VMEM((width, units), BF16),
            pltpu.SemaphoreType.DMA((n_nar, 2, 2)),
            pltpu.SemaphoreType.DMA,
        ],
        mib=60,
    )
    parts = list(parts)
    for k in range(1, n_nar):
        parts[k] = lax.ppermute(parts[k], "narrow", [(i, (i + k) % n_nar) for i in range(n_nar)])
    arrived = call(
        arrived_body, jax.ShapeDtypeStruct((8, 128), F32), [ANY] * (n_nar - 1), parts[1:], flops=HOLD
    )

    half = n_far * CAP // 2
    picked = call(
        functools.partial(pick_body, part, top),
        jax.ShapeDtypeStruct((near, half, 2 * part), BF16),
        [VMEM],
        [rows],
        flops=2 * slots * n_far * tok * part,
    )
    weight = call(
        functools.partial(weight_body, part, top),
        jax.ShapeDtypeStruct((2, slots // 2, 2 * n_far * tok), BF16),
        [VMEM],
        [rows],
    )
    rows = exchange(picked, NEAR)

    acts = call(
        functools.partial(gate_up_body, n_nar),
        jax.ShapeDtypeStruct((n_nar, slots, 2 * units), BF16),
        [VMEM] + [VMEM] * n_nar + [ANY],
        [rows] + parts + [arrived],
        flops=2 * slots * part * 2 * units * 2 * n_nar,
    )
    acts = exchange(acts, "narrow")
    inner = call(inner_body, jax.ShapeDtypeStruct((n_nar, slots, units), BF16), [VMEM], [acts])
    inner = exchange(inner, "narrow")
    outs = call(
        functools.partial(down_body, n_nar),
        jax.ShapeDtypeStruct((near, half, 2 * part), BF16),
        [VMEM] + [VMEM] * n_nar,
        [inner] + parts,
        flops=2 * slots * units * n_nar * 2 * part,
    )
    outs = exchange(outs, NEAR)
    sums = call(
        combine_body,
        jax.ShapeDtypeStruct((n_far, tok // 2, 2 * part), BF16),
        [VMEM, VMEM],
        [outs, weight],
        flops=2 * slots * 2 * 2 * n_far * tok * part,
    )
    sums = exchange(sums, FAR)
    return call(last_body, jax.ShapeDtypeStruct((tok, part), BF16), [VMEM], [sums])


def solution(mesh):
    n_grp, n_wide, n_nar = mesh.devices.shape
    fine = Mesh(mesh.devices.reshape(n_grp, 2, n_wide // 8, 2, 2, n_nar), AXES)
    return jax.shard_map(
        per_device,
        mesh=fine,
        in_specs=(
            P(WIDE, None),
            P(WIDE, None),
            P(WIDE, None),
            P(WIDE, None, ("grp", "narrow")),
            P(WIDE, None, ("grp", "narrow")),
            P(WIDE, ("grp", "narrow"), None),
        ),
        out_specs=P(WIDE, ("grp", "narrow")),
        check_vma=False,
    )
```

```python
import functools

import jax
import jax.numpy as jnp
from jax import lax
from jax.experimental import pallas as pl
from jax.experimental.pallas import tpu as pltpu
from jax.sharding import Mesh, PartitionSpec as P

CAP = 8
F32 = jnp.float32
BF16 = jnp.bfloat16
I32 = jnp.int32
FAR = "zfar"
NEAR = ("grp", "core", "ylo", "znear")
AXES = ("grp", "ylo", "zfar", "znear", "core", "narrow")
WIDE = ("ylo", "zfar", "znear", "core")
LANES = 512
HOLD = 200 * 10**9
ORDER = (2, 1, 3, 0)

VMEM = pl.BlockSpec(memory_space=pltpu.VMEM)
SMEM = pl.BlockSpec(memory_space=pltpu.SMEM)
ANY = pl.BlockSpec(memory_space=pl.ANY)
HBM = pl.BlockSpec(memory_space=pltpu.HBM)


def call(body, outs, specs, args, flops=0, scratch=(), mib=16):
    single = not isinstance(outs, list)
    outs = [outs] if single else outs
    nbytes = sum(a.size * a.dtype.itemsize for a in args) + sum(o.size * o.dtype.itemsize for o in outs)
    got = pl.pallas_call(
        body,
        out_shape=outs,
        in_specs=specs,
        out_specs=[VMEM] * len(outs),
        scratch_shapes=list(scratch),
        compiler_params=pltpu.CompilerParams(vmem_limit_bytes=mib * 1024 * 1024),
        cost_estimate=pl.CostEstimate(flops=flops, bytes_accessed=nbytes, transcendentals=0),
    )(*args)
    return got[0] if single else got


def exchange(x, axis):
    groups = {FAR: [[0, 2, 4, 6, 1, 3, 5, 7]], "narrow": [[0, 3, 1, 2]]}.get(axis)
    return lax.all_to_all(x, axis, split_axis=0, concat_axis=0, tiled=True, axis_index_groups=groups)


def place_of(index):
    return jnp.where(index == 0, 0, jnp.where(index == 3, 1, index + 1))


def rows_body(part, top, hidden_hbm, routes_hbm, gates_hbm, out_ref, wide_ref, routes_ref, gates_ref, sems):
    count, tok, lanes = out_ref.shape
    odd = lax.axis_index("grp")
    start = pl.multiple_of(lax.axis_index("narrow") * 2 * part + odd * (part // 128 * 128), 128)
    copies = [
        pltpu.make_async_copy(hidden_hbm.at[:, pl.ds(start, LANES)], wide_ref, sems.at[0]),
        pltpu.make_async_copy(routes_hbm, routes_ref, sems.at[1]),
        pltpu.make_async_copy(gates_hbm, gates_ref, sems.at[2]),
    ]
    for copy in copies:
        copy.start()
    for copy in copies:
        copy.wait()
    wide = wide_ref[...].astype(F32)
    mine = jnp.where(odd == 1, wide[:, LANES - part :], wide[:, :part])
    gates = gates_ref[...]
    high = gates.astype(BF16).astype(F32)
    extra = jnp.concatenate([routes_ref[...].astype(F32), high, gates - high], axis=0).astype(BF16)
    eye = (lax.broadcasted_iota(I32, (tok, tok), 0) == lax.broadcasted_iota(I32, (tok, tok), 1)).astype(BF16)
    extra = lax.dot_general(eye, extra, (((1,), (1,)), ((), ())), preferred_element_type=F32)
    spare = jnp.zeros((tok, lanes - part - 3 * top), F32)
    rows = jnp.concatenate([mine, extra, spare], axis=1).astype(BF16)
    for i in range(count):
        out_ref[i] = rows


def pack_body(n_nar, part, gate_hbm, up_hbm, down_hbm, *rest):
    outs = [rest[ORDER.index(k)] for k in range(n_nar)]
    down_ref, turned_ref, sems, down_sem = rest[n_nar:]
    units = gate_hbm.shape[2]
    me = lax.axis_index("narrow")
    fetch = pltpu.make_async_copy(down_hbm.at[0], down_ref, down_sem)
    fetch.start()
    copies = []
    for k in range(n_nar):
        to = lax.rem(me + k, n_nar)
        for i in range(2):
            rows = pl.ds(pl.multiple_of((to * 2 + i) * part, 64), part)
            for m, source in enumerate((gate_hbm, up_hbm)):
                place = outs[k].at[i, :, m * units : (m + 1) * units]
                copies.append(pltpu.make_async_copy(source.at[0, rows], place, sems.at[k, i, m]))
    for copy in copies:
        copy.start()
    fetch.wait()
    turned_ref[...] = jnp.transpose(down_ref[...])
    for k in range(n_nar):
        to = lax.rem(me + k, n_nar)
        for i in range(2):
            rows = pl.ds(pl.multiple_of((i * n_nar + to) * part, 64), part)
            outs[k][2, :, i * units : (i + 1) * units] = turned_ref[rows]
    for copy in copies:
        copy.wait()


def own_body(part_hbm, _, out_ref, sem):
    copy = pltpu.make_async_copy(part_hbm, out_ref, sem)
    copy.start()
    copy.wait()


def arrived_body(*refs):
    refs[-1][...] = jnp.zeros(refs[-1].shape, F32)


def slots_of(part, top, rows_ref):
    blocks, tok, _ = rows_ref.shape
    count = blocks * tok
    extra = rows_ref[...].reshape(count, LANES)[:, part : part + 3 * top]
    eye = (
        lax.broadcasted_iota(I32, (3 * top, 3 * top), 0) == lax.broadcasted_iota(I32, (3 * top, 3 * top), 1)
    ).astype(BF16)
    extra = lax.dot_general(eye, extra, (((1,), (1,)), ((), ())), preferred_element_type=F32)
    j = lax.broadcasted_iota(I32, (8, count), 0)
    z_count = 2 * lax.axis_size(FAR)
    expert = (((j // 2 % 2) * z_count + lax.axis_index(FAR) * 2 + j % 2) * 2 + j // 4).astype(F32)
    chosen = jnp.zeros((8, count), F32)
    gate = jnp.zeros((8, count), F32)
    for k in range(top):
        same = extra[k : k + 1] == expert
        chosen = jnp.where(same, 1.0, chosen)
        value = extra[top + k : top + k + 1] + extra[2 * top + k : 2 * top + k + 1]
        gate = gate + jnp.where(same, value, 0.0)
    first = lax.broadcasted_iota(I32, (count, count), 0)
    second = lax.broadcasted_iota(I32, (count, count), 1)
    before = ((first < second) & (first // tok == second // tok)).astype(BF16)
    place = jnp.dot(chosen.astype(BF16), before, preferred_element_type=F32)
    block = (lax.broadcasted_iota(I32, (8, count), 1) // tok).astype(F32)
    slot = jnp.where(chosen > 0.0, place + block * CAP, -1.0)
    want = lax.broadcasted_iota(I32, (8, blocks * CAP, count), 1).astype(F32)
    return slot[:, None, :] == want, gate


def pick_body(part, top, rows_ref, out_ref):
    near, half, _ = out_ref.shape
    near = near // 2
    hit, _ = slots_of(part, top, rows_ref)
    picker = jnp.where(hit, 1.0, 0.0).astype(BF16)
    rows = rows_ref[...].reshape(-1, LANES)[:, :part]
    sides = []
    for i in range(2):
        left = picker[:, i * half : (i + 1) * half].reshape(near * half, -1)
        sides.append(jnp.dot(left, rows, preferred_element_type=F32))
    got = jnp.concatenate(sides, axis=1).astype(BF16).reshape(near, half, 2 * part)
    out_ref[:near] = got
    out_ref[near:] = got


def weight_body(part, top, rows_ref, out_ref):
    _, half, count = out_ref.shape
    hit, gate = slots_of(part, top, rows_ref)
    weight = jnp.where(hit, gate[:, None, :], 0.0)
    high = weight.astype(BF16)
    low = (weight - high.astype(F32)).astype(BF16)
    both = jnp.concatenate([high, low], axis=2)
    near = both.shape[0]
    for i in range(2):
        side = both[:, i * (both.shape[1] // 2) : (i + 1) * (both.shape[1] // 2)]
        out_ref[i] = side.reshape(half, count)


def two_sides(rows, part):
    rows = rows.reshape(-1, 2 * part)
    return jnp.concatenate([rows[:, :part], rows[:, part:]], axis=0)


def gate_up_body(n_nar, rows_ref, *rest):
    parts, out_ref = [rest[ORDER.index(k)] for k in range(n_nar)], rest[-1]
    me = lax.axis_index("narrow")
    part = rows_ref.shape[2] // 2
    half = rows_ref.shape[0] // 2
    left = two_sides(rows_ref[:half], part)
    right = two_sides(rows_ref[half:], part)
    for k in range(n_nar):
        act = jnp.dot(left, parts[k][0], preferred_element_type=F32)
        act = act + jnp.dot(right, parts[k][1], preferred_element_type=F32)
        out_ref[place_of(lax.rem(me - k + n_nar, n_nar))] = act.astype(BF16)


def inner_body(acts_ref, out_ref):
    count, _, units = out_ref.shape
    act = sum(acts_ref[i].astype(F32) for i in range(count))
    gate, up = act[:, :units], act[:, units:]
    inner = (gate / (1.0 + jnp.exp(-gate)) * up).astype(BF16)
    for i in range(count):
        out_ref[i] = inner


def down_body(n_nar, inner_ref, *rest):
    parts, out_ref = [rest[ORDER.index(k)] for k in range(n_nar)], rest[-1]
    me = lax.axis_index("narrow")
    near = out_ref.shape[0] // 2
    units = inner_ref.shape[2]
    left = jnp.concatenate([inner_ref[place_of(lax.rem(me - k + n_nar, n_nar))] for k in range(n_nar)], axis=1)
    count = left.shape[0] // 2
    for i in range(2):
        right = jnp.concatenate([parts[k][2, :, i * units : (i + 1) * units] for k in range(n_nar)], axis=1)
        out = lax.dot_general(left, right, (((1,), (1,)), ((), ())), preferred_element_type=F32)
        out = jnp.concatenate([out[:count], out[count:]], axis=1).astype(BF16)
        out_ref[i * near : (i + 1) * near] = out.reshape(near, -1, out.shape[1])


def combine_body(rows_ref, weight_ref, out_ref):
    blocks, half, width = out_ref.shape
    near = rows_ref.shape[0] // 2
    part = width // 2
    total = 0.0
    for i in range(2):
        rows = rows_ref[i * near : (i + 1) * near].reshape(-1, width)
        for h in range(2):
            side = rows[:, h * part : (h + 1) * part]
            total = total + lax.dot_general(
                weight_ref[h], side, (((0,), (0,)), ((), ())), preferred_element_type=F32
            )
    count = total.shape[0] // 2
    total = (total[:count] + total[count:]).reshape(blocks, 2 * half, part)
    total = jnp.concatenate([total[:, :half], total[:, half:]], axis=2)
    out_ref[...] = total.astype(BF16)


def last_body(sums_ref, out_ref):
    total = sum(sums_ref[i].astype(F32) for i in range(sums_ref.shape[0]))
    half, width = total.shape
    out_ref[:half] = total[:, : width // 2].astype(BF16)
    out_ref[half:] = total[:, width // 2 :].astype(BF16)


def per_device(hidden, routes, route_gates, gate_proj, up_proj, down_proj):
    tok, width = hidden.shape
    top = routes.shape[1]
    n_grp, n_nar, n_far = lax.axis_size("grp"), lax.axis_size("narrow"), lax.axis_size(FAR)
    units = gate_proj.shape[2]
    part = width // (n_grp * n_nar)
    near = 16
    slots = 8 * n_far * CAP

    rows = call(
        functools.partial(rows_body, part, top),
        jax.ShapeDtypeStruct((n_far, tok, LANES), BF16),
        [HBM, HBM, HBM],
        [hidden, routes.T, route_gates.T],
        scratch=[
            pltpu.VMEM((tok, LANES), BF16),
            pltpu.VMEM((top, tok), I32),
            pltpu.VMEM((top, tok), F32),
            pltpu.SemaphoreType.DMA((3,)),
        ],
        mib=60,
    )
    rows = exchange(rows, FAR)

    parts = call(
        functools.partial(pack_body, n_nar, part),
        [jax.ShapeDtypeStruct((3, part, 2 * units), BF16)] * n_nar,
        [HBM, HBM, HBM],
        [gate_proj, up_proj, down_proj],
        scratch=[
            pltpu.VMEM((units, width), BF16),
            pltpu.VMEM((width, units), BF16),
            pltpu.SemaphoreType.DMA((n_nar, 2, 2)),
            pltpu.SemaphoreType.DMA,
        ],
        mib=60,
    )
    parts = [parts[ORDER.index(k)] for k in range(n_nar)]
    for k in ORDER[:-1]:
        parts[k] = lax.ppermute(parts[k], "narrow", [(i, (i + k) % n_nar) for i in range(n_nar)])
    half = n_far * CAP // 2
    picked = call(
        functools.partial(pick_body, part, top),
        jax.ShapeDtypeStruct((near, half, 2 * part), BF16),
        [VMEM],
        [rows],
        flops=2 * slots * n_far * tok * part,
    )
    weight = call(
        functools.partial(weight_body, part, top),
        jax.ShapeDtypeStruct((2, slots // 2, 2 * n_far * tok), BF16),
        [VMEM],
        [rows],
    )
    parts[0] = call(
        own_body,
        jax.ShapeDtypeStruct(parts[0].shape, BF16),
        [HBM, ANY],
        [parts[0], picked],
        scratch=[pltpu.SemaphoreType.DMA],
    )
    arrived = call(
        arrived_body, jax.ShapeDtypeStruct((8, 128), F32), [ANY] * n_nar, [parts[k] for k in ORDER], flops=HOLD
    )
    rows = exchange(picked, NEAR)

    acts = call(
        functools.partial(gate_up_body, n_nar),
        jax.ShapeDtypeStruct((n_nar, slots, 2 * units), BF16),
        [VMEM] + [VMEM] * n_nar + [ANY],
        [rows] + [parts[k] for k in ORDER] + [arrived],
        flops=2 * slots * part * 2 * units * 2 * n_nar,
    )
    acts = exchange(acts, "narrow")
    inner = call(inner_body, jax.ShapeDtypeStruct((n_nar, slots, units), BF16), [VMEM], [acts])
    inner = exchange(inner, "narrow")
    outs = call(
        functools.partial(down_body, n_nar),
        jax.ShapeDtypeStruct((near, half, 2 * part), BF16),
        [VMEM] + [VMEM] * n_nar,
        [inner] + [parts[k] for k in ORDER],
        flops=2 * slots * units * n_nar * 2 * part,
    )
    outs = exchange(outs, NEAR)
    sums = call(
        combine_body,
        jax.ShapeDtypeStruct((n_far, tok // 2, 2 * part), BF16),
        [VMEM, VMEM],
        [outs, weight],
        flops=2 * slots * 2 * 2 * n_far * tok * part,
    )
    sums = exchange(sums, FAR)
    return call(last_body, jax.ShapeDtypeStruct((tok, part), BF16), [VMEM], [sums])


def solution(mesh):
    n_grp, n_wide, n_nar = mesh.devices.shape
    fine = Mesh(mesh.devices.reshape(n_grp, 2, n_wide // 8, 2, 2, n_nar), AXES)
    return jax.shard_map(
        per_device,
        mesh=fine,
        in_specs=(
            P(WIDE, None),
            P(WIDE, None),
            P(WIDE, None),
            P(WIDE, None, ("grp", "narrow")),
            P(WIDE, None, ("grp", "narrow")),
            P(WIDE, ("grp", "narrow"), None),
        ),
        out_specs=P(WIDE, ("grp", "narrow")),
        check_vma=False,
    )
```

```python
import functools

import jax
import jax.numpy as jnp
from jax import lax
from jax.experimental import pallas as pl
from jax.experimental.pallas import tpu as pltpu
from jax.sharding import Mesh, PartitionSpec as P

CAP = 8
F32 = jnp.float32
BF16 = jnp.bfloat16
I32 = jnp.int32
FAR = "zfar"
NEAR = ("grp", "core", "ylo", "znear")
AXES = ("grp", "ylo", "zfar", "znear", "core", "narrow")
WIDE = ("ylo", "zfar", "znear", "core")
LANES = 512
HOLD = 200 * 10**9
ORDER = (2, 1, 3, 0)
FAR_ORDER = (0, 4, 1, 5, 2, 6, 3, 7)
NARROW_ORDER = (0, 1, 3, 2)

VMEM = pl.BlockSpec(memory_space=pltpu.VMEM)
SMEM = pl.BlockSpec(memory_space=pltpu.SMEM)
ANY = pl.BlockSpec(memory_space=pl.ANY)
HBM = pl.BlockSpec(memory_space=pltpu.HBM)


def call(body, outs, specs, args, flops=0, scratch=(), mib=16, place=None):
    single = not isinstance(outs, list)
    outs = [outs] if single else outs
    nbytes = sum(a.size * a.dtype.itemsize for a in args) + sum(o.size * o.dtype.itemsize for o in outs)
    got = pl.pallas_call(
        body,
        out_shape=outs,
        in_specs=specs,
        out_specs=[place or VMEM] * len(outs),
        scratch_shapes=list(scratch),
        compiler_params=pltpu.CompilerParams(vmem_limit_bytes=mib * 1024 * 1024),
        cost_estimate=pl.CostEstimate(flops=flops, bytes_accessed=nbytes, transcendentals=0),
    )(*args)
    return got[0] if single else got


def exchange(x, axis):
    groups = {FAR: [list(FAR_ORDER)], "narrow": [list(NARROW_ORDER)]}.get(axis)
    return lax.all_to_all(x, axis, split_axis=0, concat_axis=0, tiled=True, axis_index_groups=groups)


def place_of(index):
    return sum(jnp.where(index == device, at, 0) for at, device in enumerate(NARROW_ORDER))


def rows_body(part, top, hidden_hbm, routes_hbm, gates_hbm, out_ref, wide_ref, routes_ref, gates_ref, sems):
    count, tok, lanes = out_ref.shape
    odd = lax.axis_index("grp")
    start = pl.multiple_of(lax.axis_index("narrow") * 2 * part + odd * (part // 128 * 128), 128)
    copies = [
        pltpu.make_async_copy(hidden_hbm.at[:, pl.ds(start, LANES)], wide_ref, sems.at[0]),
        pltpu.make_async_copy(routes_hbm, routes_ref, sems.at[1]),
        pltpu.make_async_copy(gates_hbm, gates_ref, sems.at[2]),
    ]
    for copy in copies:
        copy.start()
    for copy in copies:
        copy.wait()
    wide = wide_ref[...].astype(F32)
    mine = jnp.where(odd == 1, wide[:, LANES - part :], wide[:, :part])
    gates = gates_ref[...]
    high = gates.astype(BF16).astype(F32)
    extra = jnp.concatenate([routes_ref[...].astype(F32), high, gates - high], axis=0).astype(BF16)
    eye = (lax.broadcasted_iota(I32, (tok, tok), 0) == lax.broadcasted_iota(I32, (tok, tok), 1)).astype(BF16)
    extra = lax.dot_general(eye, extra, (((1,), (1,)), ((), ())), preferred_element_type=F32)
    spare = jnp.zeros((tok, lanes - part - 3 * top), F32)
    rows = jnp.concatenate([mine, extra, spare], axis=1).astype(BF16)
    for i in range(count):
        out_ref[i] = rows


def pack_body(n_nar, part, gate_hbm, up_hbm, down_hbm, *rest):
    outs = [rest[ORDER.index(k)] for k in range(n_nar)]
    down_ref, turned_ref, held_ref, sems, turned_sems, out_sems, down_sem = rest[n_nar:]
    units = gate_hbm.shape[2]
    me = lax.axis_index("narrow")
    fetch = pltpu.make_async_copy(down_hbm.at[0], down_ref, down_sem)
    fetch.start()
    copies = []
    for k in ORDER:
        to = lax.rem(me + k, n_nar)
        for i in range(2):
            rows = pl.ds(pl.multiple_of((to * 2 + i) * part, 64), part)
            for m, source in enumerate((gate_hbm, up_hbm)):
                place = held_ref.at[k, i, :, m * units : (m + 1) * units]
                copies.append(pltpu.make_async_copy(source.at[0, rows], place, sems.at[k, i, m]))
    for copy in copies:
        copy.start()
    fetch.wait()
    turned_ref[...] = jnp.transpose(down_ref[...])
    sends = []
    for at, k in enumerate(ORDER):
        to = lax.rem(me + k, n_nar)
        for copy in copies[4 * at : 4 * at + 4]:
            copy.wait()
        sends.append(pltpu.make_async_copy(held_ref.at[k, :2], outs[k].at[:2], out_sems.at[k]))
        sends[-1].start()
        for i in range(2):
            rows = pl.ds(pl.multiple_of((i * n_nar + to) * part, 64), part)
            held_ref[k, 2, :, i * units : (i + 1) * units] = turned_ref[rows]
        sends.append(pltpu.make_async_copy(held_ref.at[k, 2], outs[k].at[2], turned_sems.at[k]))
        sends[-1].start()
    for copy in sends:
        copy.wait()


def own_body(part_hbm, _, out_ref, sem):
    copy = pltpu.make_async_copy(part_hbm, out_ref, sem)
    copy.start()
    copy.wait()


def arrived_body(*refs):
    refs[-1][...] = jnp.zeros(refs[-1].shape, F32)


def slots_of(part, top, rows_ref):
    blocks, tok, _ = rows_ref.shape
    count = blocks * tok
    extra = rows_ref[...].reshape(count, LANES)[:, part : part + 3 * top]
    eye = (
        lax.broadcasted_iota(I32, (3 * top, 3 * top), 0) == lax.broadcasted_iota(I32, (3 * top, 3 * top), 1)
    ).astype(BF16)
    extra = lax.dot_general(eye, extra, (((1,), (1,)), ((), ())), preferred_element_type=F32)
    j = lax.broadcasted_iota(I32, (8, count), 0)
    z_count = 2 * lax.axis_size(FAR)
    expert = (((j // 2 % 2) * z_count + lax.axis_index(FAR) * 2 + j % 2) * 2 + j // 4).astype(F32)
    chosen = jnp.zeros((8, count), F32)
    gate = jnp.zeros((8, count), F32)
    for k in range(top):
        same = extra[k : k + 1] == expert
        chosen = jnp.where(same, 1.0, chosen)
        value = extra[top + k : top + k + 1] + extra[2 * top + k : 2 * top + k + 1]
        gate = gate + jnp.where(same, value, 0.0)
    first = lax.broadcasted_iota(I32, (count, count), 0)
    second = lax.broadcasted_iota(I32, (count, count), 1)
    before = ((first < second) & (first // tok == second // tok)).astype(BF16)
    place = jnp.dot(chosen.astype(BF16), before, preferred_element_type=F32)
    block = (lax.broadcasted_iota(I32, (8, count), 1) // tok).astype(F32)
    slot = jnp.where(chosen > 0.0, place + block * CAP, -1.0)
    want = lax.broadcasted_iota(I32, (8, blocks * CAP, count), 1).astype(F32)
    return slot[:, None, :] == want, gate


def pick_body(part, top, rows_ref, out_ref):
    near, half, _ = out_ref.shape
    near = near // 2
    hit, _ = slots_of(part, top, rows_ref)
    picker = jnp.where(hit, 1.0, 0.0).astype(BF16)
    rows = rows_ref[...].reshape(-1, LANES)[:, :part]
    sides = []
    for i in range(2):
        left = picker[:, i * half : (i + 1) * half].reshape(near * half, -1)
        sides.append(jnp.dot(left, rows, preferred_element_type=F32))
    got = jnp.concatenate(sides, axis=1).astype(BF16).reshape(near, half, 2 * part)
    out_ref[:near] = got
    out_ref[near:] = got


def weight_body(part, top, rows_ref, out_ref):
    _, half, count = out_ref.shape
    hit, gate = slots_of(part, top, rows_ref)
    weight = jnp.where(hit, gate[:, None, :], 0.0)
    high = weight.astype(BF16)
    low = (weight - high.astype(F32)).astype(BF16)
    both = jnp.concatenate([high, low], axis=2)
    near = both.shape[0]
    for i in range(2):
        side = both[:, i * (both.shape[1] // 2) : (i + 1) * (both.shape[1] // 2)]
        out_ref[i] = side.reshape(half, count)


def two_sides(rows, part):
    rows = rows.reshape(-1, 2 * part)
    return jnp.concatenate([rows[:, :part], rows[:, part:]], axis=0)


def gate_up_body(n_nar, rows_ref, *rest):
    parts, out_ref = [rest[ORDER.index(k)] for k in range(n_nar)], rest[-1]
    me = lax.axis_index("narrow")
    part = rows_ref.shape[2] // 2
    half = rows_ref.shape[0] // 2
    left = two_sides(rows_ref[:half], part)
    right = two_sides(rows_ref[half:], part)
    for k in range(n_nar):
        act = jnp.dot(left, parts[k][0], preferred_element_type=F32)
        act = act + jnp.dot(right, parts[k][1], preferred_element_type=F32)
        out_ref[place_of(lax.rem(me - k + n_nar, n_nar))] = act.astype(BF16)


def inner_body(acts_ref, out_ref):
    count, _, units = out_ref.shape
    act = sum(acts_ref[i].astype(F32) for i in range(count))
    gate, up = act[:, :units], act[:, units:]
    inner = (gate / (1.0 + jnp.exp(-gate)) * up).astype(BF16)
    for i in range(count):
        out_ref[i] = inner


def down_body(n_nar, inner_ref, *rest):
    parts, out_ref = [rest[ORDER.index(k)] for k in range(n_nar)], rest[-1]
    me = lax.axis_index("narrow")
    near = out_ref.shape[0] // 2
    units = inner_ref.shape[2]
    left = jnp.concatenate([inner_ref[place_of(lax.rem(me - k + n_nar, n_nar))] for k in range(n_nar)], axis=1)
    count = left.shape[0] // 2
    for i in range(2):
        right = jnp.concatenate([parts[k][2, :, i * units : (i + 1) * units] for k in range(n_nar)], axis=1)
        out = lax.dot_general(left, right, (((1,), (1,)), ((), ())), preferred_element_type=F32)
        out = jnp.concatenate([out[:count], out[count:]], axis=1).astype(BF16)
        out_ref[i * near : (i + 1) * near] = out.reshape(near, -1, out.shape[1])


def combine_body(rows_ref, weight_ref, out_ref):
    blocks, half, width = out_ref.shape
    near = rows_ref.shape[0] // 2
    part = width // 2
    total = 0.0
    for i in range(2):
        rows = rows_ref[i * near : (i + 1) * near].reshape(-1, width)
        for h in range(2):
            side = rows[:, h * part : (h + 1) * part]
            total = total + lax.dot_general(
                weight_ref[h], side, (((0,), (0,)), ((), ())), preferred_element_type=F32
            )
    count = total.shape[0] // 2
    total = (total[:count] + total[count:]).reshape(blocks, 2 * half, part)
    total = jnp.concatenate([total[:, :half], total[:, half:]], axis=2)
    out_ref[...] = total.astype(BF16)


def last_body(sums_ref, out_ref):
    total = sum(sums_ref[i].astype(F32) for i in range(sums_ref.shape[0]))
    half, width = total.shape
    out_ref[:half] = total[:, : width // 2].astype(BF16)
    out_ref[half:] = total[:, width // 2 :].astype(BF16)


def per_device(hidden, routes, route_gates, gate_proj, up_proj, down_proj):
    tok, width = hidden.shape
    top = routes.shape[1]
    n_grp, n_nar, n_far = lax.axis_size("grp"), lax.axis_size("narrow"), lax.axis_size(FAR)
    units = gate_proj.shape[2]
    part = width // (n_grp * n_nar)
    near = 16
    slots = 8 * n_far * CAP

    rows = call(
        functools.partial(rows_body, part, top),
        jax.ShapeDtypeStruct((n_far, tok, LANES), BF16),
        [HBM, HBM, HBM],
        [hidden, routes.T, route_gates.T],
        scratch=[
            pltpu.VMEM((tok, LANES), BF16),
            pltpu.VMEM((top, tok), I32),
            pltpu.VMEM((top, tok), F32),
            pltpu.SemaphoreType.DMA((3,)),
        ],
        mib=60,
    )
    rows = exchange(rows, FAR)

    parts = call(
        functools.partial(pack_body, n_nar, part),
        [jax.ShapeDtypeStruct((3, part, 2 * units), BF16)] * n_nar,
        [HBM, HBM, HBM],
        [gate_proj, up_proj, down_proj],
        place=HBM,
        scratch=[
            pltpu.VMEM((units, width), BF16),
            pltpu.VMEM((width, units), BF16),
            pltpu.VMEM((n_nar, 3, part, 2 * units), BF16),
            pltpu.SemaphoreType.DMA((n_nar, 2, 2)),
            pltpu.SemaphoreType.DMA((n_nar,)),
            pltpu.SemaphoreType.DMA((n_nar,)),
            pltpu.SemaphoreType.DMA,
        ],
        mib=60,
    )
    parts = [parts[ORDER.index(k)] for k in range(n_nar)]
    for k in ORDER[:-1]:
        parts[k] = lax.ppermute(parts[k], "narrow", [(i, (i + k) % n_nar) for i in range(n_nar)])
    half = n_far * CAP // 2
    picked = call(
        functools.partial(pick_body, part, top),
        jax.ShapeDtypeStruct((near, half, 2 * part), BF16),
        [VMEM],
        [rows],
        flops=2 * slots * n_far * tok * part,
    )
    weight = call(
        functools.partial(weight_body, part, top),
        jax.ShapeDtypeStruct((2, slots // 2, 2 * n_far * tok), BF16),
        [VMEM],
        [rows],
    )
    parts[0] = call(
        own_body,
        jax.ShapeDtypeStruct(parts[0].shape, BF16),
        [HBM, ANY],
        [parts[0], picked],
        scratch=[pltpu.SemaphoreType.DMA],
    )
    arrived = call(
        arrived_body, jax.ShapeDtypeStruct((8, 128), F32), [ANY] * n_nar, [parts[k] for k in ORDER], flops=HOLD
    )
    rows = exchange(picked, NEAR)

    acts = call(
        functools.partial(gate_up_body, n_nar),
        jax.ShapeDtypeStruct((n_nar, slots, 2 * units), BF16),
        [VMEM] + [VMEM] * n_nar + [ANY],
        [rows] + [parts[k] for k in ORDER] + [arrived],
        flops=2 * slots * part * 2 * units * 2 * n_nar,
    )
    acts = exchange(acts, "narrow")
    inner = call(inner_body, jax.ShapeDtypeStruct((n_nar, slots, units), BF16), [VMEM], [acts])
    inner = exchange(inner, "narrow")
    outs = call(
        functools.partial(down_body, n_nar),
        jax.ShapeDtypeStruct((near, half, 2 * part), BF16),
        [VMEM] + [VMEM] * n_nar,
        [inner] + [parts[k] for k in ORDER],
        flops=2 * slots * units * n_nar * 2 * part,
    )
    outs = exchange(outs, NEAR)
    sums = call(
        combine_body,
        jax.ShapeDtypeStruct((n_far, tok // 2, 2 * part), BF16),
        [VMEM, VMEM],
        [outs, weight],
        flops=2 * slots * 2 * 2 * n_far * tok * part,
    )
    sums = exchange(sums, FAR)
    return call(last_body, jax.ShapeDtypeStruct((tok, part), BF16), [VMEM], [sums])


def solution(mesh):
    n_grp, n_wide, n_nar = mesh.devices.shape
    fine = Mesh(mesh.devices.reshape(n_grp, 2, n_wide // 8, 2, 2, n_nar), AXES)
    return jax.shard_map(
        per_device,
        mesh=fine,
        in_specs=(
            P(WIDE, None),
            P(WIDE, None),
            P(WIDE, None),
            P(WIDE, None, ("grp", "narrow")),
            P(WIDE, None, ("grp", "narrow")),
            P(WIDE, ("grp", "narrow"), None),
        ),
        out_specs=P(WIDE, ("grp", "narrow")),
        check_vma=False,
    )
```

```python
import functools

import jax
import jax.numpy as jnp
from jax import lax
from jax.experimental import pallas as pl
from jax.experimental.pallas import tpu as pltpu
from jax.sharding import Mesh, PartitionSpec as P

CAP = 8
F32 = jnp.float32
BF16 = jnp.bfloat16
I32 = jnp.int32
FAR = "zfar"
NEAR = ("grp", "core", "ylo", "znear")
AXES = ("grp", "ylo", "zfar", "znear", "core", "narrow")
WIDE = ("ylo", "zfar", "znear", "core")
LANES = 512
HOLD = 200 * 10**9
ORDER = (2, 1, 3, 0)
FAR_ORDER = (0, 4, 1, 5, 2, 6, 3, 7)
NARROW_ORDER = (0, 1, 3, 2)

VMEM = pl.BlockSpec(memory_space=pltpu.VMEM)
SMEM = pl.BlockSpec(memory_space=pltpu.SMEM)
ANY = pl.BlockSpec(memory_space=pl.ANY)
HBM = pl.BlockSpec(memory_space=pltpu.HBM)


def call(body, outs, specs, args, flops=0, scratch=(), mib=16, place=None):
    single = not isinstance(outs, list)
    outs = [outs] if single else outs
    nbytes = sum(a.size * a.dtype.itemsize for a in args) + sum(o.size * o.dtype.itemsize for o in outs)
    got = pl.pallas_call(
        body,
        out_shape=outs,
        in_specs=specs,
        out_specs=[place or VMEM] * len(outs),
        scratch_shapes=list(scratch),
        compiler_params=pltpu.CompilerParams(vmem_limit_bytes=mib * 1024 * 1024),
        cost_estimate=pl.CostEstimate(flops=flops, bytes_accessed=nbytes, transcendentals=0),
    )(*args)
    return got[0] if single else got


def exchange(x, axis):
    groups = {FAR: [list(FAR_ORDER)], "narrow": [list(NARROW_ORDER)]}.get(axis)
    return lax.all_to_all(x, axis, split_axis=0, concat_axis=0, tiled=True, axis_index_groups=groups)


def place_of(index):
    return sum(jnp.where(index == device, at, 0) for at, device in enumerate(NARROW_ORDER))


def rows_body(part, top, hidden_hbm, routes_hbm, gates_hbm, out_ref, wide_ref, routes_ref, gates_ref, sems):
    count, tok, lanes = out_ref.shape
    odd = lax.axis_index("grp")
    start = pl.multiple_of(lax.axis_index("narrow") * 2 * part + odd * (part // 128 * 128), 128)
    copies = [
        pltpu.make_async_copy(hidden_hbm.at[:, pl.ds(start, LANES)], wide_ref, sems.at[0]),
        pltpu.make_async_copy(routes_hbm, routes_ref, sems.at[1]),
        pltpu.make_async_copy(gates_hbm, gates_ref, sems.at[2]),
    ]
    for copy in copies:
        copy.start()
    for copy in copies:
        copy.wait()
    wide = wide_ref[...].astype(F32)
    mine = jnp.where(odd == 1, wide[:, LANES - part :], wide[:, :part])
    gates = gates_ref[...]
    high = gates.astype(BF16).astype(F32)
    extra = jnp.concatenate([routes_ref[...].astype(F32), high, gates - high], axis=0).astype(BF16)
    eye = (lax.broadcasted_iota(I32, (tok, tok), 0) == lax.broadcasted_iota(I32, (tok, tok), 1)).astype(BF16)
    extra = lax.dot_general(eye, extra, (((1,), (1,)), ((), ())), preferred_element_type=F32)
    spare = jnp.zeros((tok, lanes - part - 3 * top), F32)
    rows = jnp.concatenate([mine, extra, spare], axis=1).astype(BF16)
    for i in range(count):
        out_ref[i] = rows


def pack_body(n_nar, part, gate_hbm, up_hbm, down_hbm, *rest):
    outs = [rest[ORDER.index(k)] for k in range(n_nar)]
    down_ref, turned_ref, held_ref, sems, turned_sems, out_sems, down_sem = rest[n_nar:]
    units = gate_hbm.shape[2]
    me = lax.axis_index("narrow")
    fetch = pltpu.make_async_copy(down_hbm.at[0], down_ref, down_sem)
    fetch.start()
    copies = []
    for k in ORDER:
        to = lax.rem(me + k, n_nar)
        for i in range(2):
            rows = pl.ds(pl.multiple_of((to * 2 + i) * part, 64), part)
            for m, source in enumerate((gate_hbm, up_hbm)):
                place = held_ref.at[k, i, :, m * units : (m + 1) * units]
                copies.append(pltpu.make_async_copy(source.at[0, rows], place, sems.at[k, i, m]))
    for copy in copies:
        copy.start()
    fetch.wait()
    turned_ref[...] = jnp.transpose(down_ref[...])
    sends = []
    for at, k in enumerate(ORDER):
        to = lax.rem(me + k, n_nar)
        for copy in copies[4 * at : 4 * at + 4]:
            copy.wait()
        sends.append(pltpu.make_async_copy(held_ref.at[k, :2], outs[k].at[:2], out_sems.at[k]))
        sends[-1].start()
        for i in range(2):
            rows = pl.ds(pl.multiple_of((i * n_nar + to) * part, 64), part)
            held_ref[k, 2, :, i * units : (i + 1) * units] = turned_ref[rows]
        sends.append(pltpu.make_async_copy(held_ref.at[k, 2], outs[k].at[2], turned_sems.at[k]))
        sends[-1].start()
    for copy in sends:
        copy.wait()


def own_body(part_hbm, _, out_ref, sem):
    copy = pltpu.make_async_copy(part_hbm, out_ref, sem)
    copy.start()
    copy.wait()


def arrived_body(*refs):
    refs[-1][...] = jnp.zeros(refs[-1].shape, F32)


def slots_of(part, top, rows_ref):
    blocks, tok, _ = rows_ref.shape
    count = blocks * tok
    extra = rows_ref[...].reshape(count, LANES)[:, part : part + 3 * top]
    eye = (
        lax.broadcasted_iota(I32, (3 * top, 3 * top), 0) == lax.broadcasted_iota(I32, (3 * top, 3 * top), 1)
    ).astype(BF16)
    extra = lax.dot_general(eye, extra, (((1,), (1,)), ((), ())), preferred_element_type=F32)
    j = lax.broadcasted_iota(I32, (8, count), 0)
    z_count = 2 * lax.axis_size(FAR)
    expert = (((j // 2 % 2) * z_count + lax.axis_index(FAR) * 2 + j % 2) * 2 + j // 4).astype(F32)
    chosen = jnp.zeros((8, count), F32)
    gate = jnp.zeros((8, count), F32)
    for k in range(top):
        same = extra[k : k + 1] == expert
        chosen = jnp.where(same, 1.0, chosen)
        value = extra[top + k : top + k + 1] + extra[2 * top + k : 2 * top + k + 1]
        gate = gate + jnp.where(same, value, 0.0)
    first = lax.broadcasted_iota(I32, (count, count), 0)
    second = lax.broadcasted_iota(I32, (count, count), 1)
    before = ((first < second) & (first // tok == second // tok)).astype(BF16)
    place = jnp.dot(chosen.astype(BF16), before, preferred_element_type=F32)
    block = (lax.broadcasted_iota(I32, (8, count), 1) // tok).astype(F32)
    slot = jnp.where(chosen > 0.0, place + block * CAP, -1.0)
    want = lax.broadcasted_iota(I32, (8, blocks * CAP, count), 1).astype(F32)
    return slot[:, None, :] == want, gate


def pick_body(part, top, rows_ref, out_ref):
    near, half, _ = out_ref.shape
    near = near // 2
    hit, _ = slots_of(part, top, rows_ref)
    picker = jnp.where(hit, 1.0, 0.0).astype(BF16)
    rows = rows_ref[...].reshape(-1, LANES)[:, :part]
    sides = []
    for i in range(2):
        left = picker[:, i * half : (i + 1) * half].reshape(near * half, -1)
        sides.append(jnp.dot(left, rows, preferred_element_type=F32))
    got = jnp.concatenate(sides, axis=1).astype(BF16).reshape(near, half, 2 * part)
    out_ref[:near] = got
    out_ref[near:] = got


def weight_body(part, top, rows_ref, out_ref):
    _, half, count = out_ref.shape
    hit, gate = slots_of(part, top, rows_ref)
    weight = jnp.where(hit, gate[:, None, :], 0.0)
    high = weight.astype(BF16)
    low = (weight - high.astype(F32)).astype(BF16)
    both = jnp.concatenate([high, low], axis=2)
    near = both.shape[0]
    for i in range(2):
        side = both[:, i * (both.shape[1] // 2) : (i + 1) * (both.shape[1] // 2)]
        out_ref[i] = side.reshape(half, count)


def two_sides(rows, part):
    rows = rows.reshape(-1, 2 * part)
    return jnp.concatenate([rows[:, :part], rows[:, part:]], axis=0)


def gate_up_body(n_nar, rows_ref, *rest):
    parts, out_ref = [rest[ORDER.index(k)] for k in range(n_nar)], rest[-1]
    me = lax.axis_index("narrow")
    part = rows_ref.shape[2] // 2
    half = rows_ref.shape[0] // 2
    left = two_sides(rows_ref[:half], part)
    right = two_sides(rows_ref[half:], part)
    for k in range(n_nar):
        act = jnp.dot(left, parts[k][0], preferred_element_type=F32)
        act = act + jnp.dot(right, parts[k][1], preferred_element_type=F32)
        out_ref[place_of(lax.rem(me - k + n_nar, n_nar))] = act.astype(BF16)


def inner_body(acts_ref, out_ref):
    count, _, units = out_ref.shape
    act = sum(acts_ref[i].astype(F32) for i in range(count))
    gate, up = act[:, :units], act[:, units:]
    inner = (gate / (1.0 + jnp.exp(-gate)) * up).astype(BF16)
    for i in range(count):
        out_ref[i] = inner


def down_body(n_nar, inner_ref, *rest):
    parts, out_ref = [rest[ORDER.index(k)] for k in range(n_nar)], rest[-1]
    me = lax.axis_index("narrow")
    near = out_ref.shape[0] // 2
    units = inner_ref.shape[2]
    left = jnp.concatenate([inner_ref[place_of(lax.rem(me - k + n_nar, n_nar))] for k in range(n_nar)], axis=1)
    count = left.shape[0] // 2
    for i in range(2):
        right = jnp.concatenate([parts[k][2, :, i * units : (i + 1) * units] for k in range(n_nar)], axis=1)
        out = lax.dot_general(left, right, (((1,), (1,)), ((), ())), preferred_element_type=F32)
        out = jnp.concatenate([out[:count], out[count:]], axis=1).astype(BF16)
        out_ref[i * near : (i + 1) * near] = out.reshape(near, -1, out.shape[1])


def combine_body(rows_ref, weight_ref, out_ref):
    blocks, half, width = out_ref.shape
    near = rows_ref.shape[0] // 2
    part = width // 2
    total = 0.0
    for i in range(2):
        rows = rows_ref[i * near : (i + 1) * near].reshape(-1, width)
        for h in range(2):
            side = rows[:, h * part : (h + 1) * part]
            total = total + lax.dot_general(
                weight_ref[h], side, (((0,), (0,)), ((), ())), preferred_element_type=F32
            )
    count = total.shape[0] // 2
    total = (total[:count] + total[count:]).reshape(blocks, 2 * half, part)
    total = jnp.concatenate([total[:, :half], total[:, half:]], axis=2)
    out_ref[...] = total.astype(BF16)


def last_body(sums_ref, out_ref):
    total = sum(sums_ref[i].astype(F32) for i in range(sums_ref.shape[0]))
    half, width = total.shape
    out_ref[:half] = total[:, : width // 2].astype(BF16)
    out_ref[half:] = total[:, width // 2 :].astype(BF16)


def per_device(hidden, routes, route_gates, gate_proj, up_proj, down_proj):
    tok, width = hidden.shape
    top = routes.shape[1]
    n_grp, n_nar, n_far = lax.axis_size("grp"), lax.axis_size("narrow"), lax.axis_size(FAR)
    units = gate_proj.shape[2]
    part = width // (n_grp * n_nar)
    near = 16
    slots = 8 * n_far * CAP

    rows = call(
        functools.partial(rows_body, part, top),
        jax.ShapeDtypeStruct((n_far, tok, LANES), BF16),
        [HBM, HBM, HBM],
        [hidden, routes.T, route_gates.T],
        scratch=[
            pltpu.VMEM((tok, LANES), BF16),
            pltpu.VMEM((top, tok), I32),
            pltpu.VMEM((top, tok), F32),
            pltpu.SemaphoreType.DMA((3,)),
        ],
        mib=60,
    )
    rows = exchange(rows, FAR)

    parts = call(
        functools.partial(pack_body, n_nar, part),
        [jax.ShapeDtypeStruct((3, part, 2 * units), BF16)] * n_nar,
        [HBM, HBM, HBM],
        [gate_proj, up_proj, down_proj],
        place=HBM,
        scratch=[
            pltpu.VMEM((units, width), BF16),
            pltpu.VMEM((width, units), BF16),
            pltpu.VMEM((n_nar, 3, part, 2 * units), BF16),
            pltpu.SemaphoreType.DMA((n_nar, 2, 2)),
            pltpu.SemaphoreType.DMA((n_nar,)),
            pltpu.SemaphoreType.DMA((n_nar,)),
            pltpu.SemaphoreType.DMA,
        ],
        mib=60,
    )
    parts = [parts[ORDER.index(k)] for k in range(n_nar)]
    for k in ORDER[:-1]:
        parts[k] = lax.ppermute(parts[k], "narrow", [(i, (i + k) % n_nar) for i in range(n_nar)])
    half = n_far * CAP // 2
    picked = call(
        functools.partial(pick_body, part, top),
        jax.ShapeDtypeStruct((near, half, 2 * part), BF16),
        [VMEM],
        [rows],
        flops=2 * slots * n_far * tok * part,
    )
    weight = call(
        functools.partial(weight_body, part, top),
        jax.ShapeDtypeStruct((2, slots // 2, 2 * n_far * tok), BF16),
        [VMEM],
        [rows],
    )
    parts[0] = call(
        own_body,
        jax.ShapeDtypeStruct(parts[0].shape, BF16),
        [HBM, ANY],
        [parts[0], picked],
        scratch=[pltpu.SemaphoreType.DMA],
    )
    arrived = call(
        arrived_body, jax.ShapeDtypeStruct((8, 128), F32), [ANY] * (n_nar + 1), [weight] + [parts[k] for k in ORDER], flops=HOLD
    )
    rows = exchange(picked, NEAR)

    acts = call(
        functools.partial(gate_up_body, n_nar),
        jax.ShapeDtypeStruct((n_nar, slots, 2 * units), BF16),
        [VMEM] + [VMEM] * n_nar + [ANY],
        [rows] + [parts[k] for k in ORDER] + [arrived],
        flops=2 * slots * part * 2 * units * 2 * n_nar,
    )
    acts = exchange(acts, "narrow")
    inner = call(inner_body, jax.ShapeDtypeStruct((n_nar, slots, units), BF16), [VMEM], [acts])
    inner = exchange(inner, "narrow")
    outs = call(
        functools.partial(down_body, n_nar),
        jax.ShapeDtypeStruct((near, half, 2 * part), BF16),
        [VMEM] + [VMEM] * n_nar,
        [inner] + [parts[k] for k in ORDER],
        flops=2 * slots * units * n_nar * 2 * part,
    )
    outs = exchange(outs, NEAR)
    sums = call(
        combine_body,
        jax.ShapeDtypeStruct((n_far, tok // 2, 2 * part), BF16),
        [VMEM, VMEM],
        [outs, weight],
        flops=2 * slots * 2 * 2 * n_far * tok * part,
    )
    sums = exchange(sums, FAR)
    return call(last_body, jax.ShapeDtypeStruct((tok, part), BF16), [VMEM], [sums])


def solution(mesh):
    n_grp, n_wide, n_nar = mesh.devices.shape
    fine = Mesh(mesh.devices.reshape(n_grp, 2, n_wide // 8, 2, 2, n_nar), AXES)
    return jax.shard_map(
        per_device,
        mesh=fine,
        in_specs=(
            P(WIDE, None),
            P(WIDE, None),
            P(WIDE, None),
            P(WIDE, None, ("grp", "narrow")),
            P(WIDE, None, ("grp", "narrow")),
            P(WIDE, ("grp", "narrow"), None),
        ),
        out_specs=P(WIDE, ("grp", "narrow")),
        check_vma=False,
    )
```

```python
import functools

import jax
import jax.numpy as jnp
from jax import lax
from jax.experimental import pallas as pl
from jax.experimental.pallas import tpu as pltpu
from jax.sharding import Mesh, PartitionSpec as P

CAP = 8
F32 = jnp.float32
BF16 = jnp.bfloat16
I32 = jnp.int32
FAR = "zfar"
NEAR = ("grp", "core", "ylo", "znear")
AXES = ("grp", "ylo", "zfar", "znear", "core", "narrow")
WIDE = ("ylo", "zfar", "znear", "core")
LANES = 512
HOLD = 200 * 10**9
ORDER = (2, 1, 3, 0)
FAR_ORDER = (0, 6, 3, 1, 7, 4, 2, 5)
NARROW_ORDER = (0, 1, 3, 2)

VMEM = pl.BlockSpec(memory_space=pltpu.VMEM)
SMEM = pl.BlockSpec(memory_space=pltpu.SMEM)
ANY = pl.BlockSpec(memory_space=pl.ANY)
HBM = pl.BlockSpec(memory_space=pltpu.HBM)


def call(body, outs, specs, args, flops=0, scratch=(), mib=16, place=None):
    single = not isinstance(outs, list)
    outs = [outs] if single else outs
    nbytes = sum(a.size * a.dtype.itemsize for a in args) + sum(o.size * o.dtype.itemsize for o in outs)
    got = pl.pallas_call(
        body,
        out_shape=outs,
        in_specs=specs,
        out_specs=[place or VMEM] * len(outs),
        scratch_shapes=list(scratch),
        compiler_params=pltpu.CompilerParams(vmem_limit_bytes=mib * 1024 * 1024),
        cost_estimate=pl.CostEstimate(flops=flops, bytes_accessed=nbytes, transcendentals=0),
    )(*args)
    return got[0] if single else got


def exchange(x, axis):
    groups = {FAR: [list(FAR_ORDER)], "narrow": [list(NARROW_ORDER)]}.get(axis)
    return lax.all_to_all(x, axis, split_axis=0, concat_axis=0, tiled=True, axis_index_groups=groups)


def place_of(index):
    return sum(jnp.where(index == device, at, 0) for at, device in enumerate(NARROW_ORDER))


def rows_body(part, top, hidden_hbm, routes_hbm, gates_hbm, out_ref, wide_ref, routes_ref, gates_ref, sems):
    count, tok, lanes = out_ref.shape
    odd = lax.axis_index("grp")
    start = pl.multiple_of(lax.axis_index("narrow") * 2 * part + odd * (part // 128 * 128), 128)
    copies = [
        pltpu.make_async_copy(hidden_hbm.at[:, pl.ds(start, LANES)], wide_ref, sems.at[0]),
        pltpu.make_async_copy(routes_hbm, routes_ref, sems.at[1]),
        pltpu.make_async_copy(gates_hbm, gates_ref, sems.at[2]),
    ]
    for copy in copies:
        copy.start()
    for copy in copies:
        copy.wait()
    wide = wide_ref[...].astype(F32)
    mine = jnp.where(odd == 1, wide[:, LANES - part :], wide[:, :part])
    gates = gates_ref[...]
    high = gates.astype(BF16).astype(F32)
    extra = jnp.concatenate([routes_ref[...].astype(F32), high, gates - high], axis=0).astype(BF16)
    eye = (lax.broadcasted_iota(I32, (tok, tok), 0) == lax.broadcasted_iota(I32, (tok, tok), 1)).astype(BF16)
    extra = lax.dot_general(eye, extra, (((1,), (1,)), ((), ())), preferred_element_type=F32)
    spare = jnp.zeros((tok, lanes - part - 3 * top), F32)
    rows = jnp.concatenate([mine, extra, spare], axis=1).astype(BF16)
    for i in range(count):
        out_ref[i] = rows


def pack_body(n_nar, part, gate_hbm, up_hbm, down_hbm, *rest):
    outs = [rest[ORDER.index(k)] for k in range(n_nar)]
    down_ref, turned_ref, held_ref, sems, turned_sems, out_sems, down_sem = rest[n_nar:]
    units = gate_hbm.shape[2]
    me = lax.axis_index("narrow")
    fetch = pltpu.make_async_copy(down_hbm.at[0], down_ref, down_sem)
    fetch.start()
    copies = []
    for k in ORDER:
        to = lax.rem(me + k, n_nar)
        for i in range(2):
            rows = pl.ds(pl.multiple_of((to * 2 + i) * part, 64), part)
            for m, source in enumerate((gate_hbm, up_hbm)):
                place = held_ref.at[k, i, :, m * units : (m + 1) * units]
                copies.append(pltpu.make_async_copy(source.at[0, rows], place, sems.at[k, i, m]))
    for copy in copies:
        copy.start()
    fetch.wait()
    turned_ref[...] = jnp.transpose(down_ref[...])
    sends = []
    for at, k in enumerate(ORDER):
        to = lax.rem(me + k, n_nar)
        for copy in copies[4 * at : 4 * at + 4]:
            copy.wait()
        sends.append(pltpu.make_async_copy(held_ref.at[k, :2], outs[k].at[:2], out_sems.at[k]))
        sends[-1].start()
        for i in range(2):
            rows = pl.ds(pl.multiple_of((i * n_nar + to) * part, 64), part)
            held_ref[k, 2, :, i * units : (i + 1) * units] = turned_ref[rows]
        sends.append(pltpu.make_async_copy(held_ref.at[k, 2], outs[k].at[2], turned_sems.at[k]))
        sends[-1].start()
    for copy in sends:
        copy.wait()


def own_body(part_hbm, _, out_ref, sem):
    copy = pltpu.make_async_copy(part_hbm, out_ref, sem)
    copy.start()
    copy.wait()


def arrived_body(*refs):
    refs[-1][...] = jnp.zeros(refs[-1].shape, F32)


def slots_of(part, top, rows_ref):
    blocks, tok, _ = rows_ref.shape
    count = blocks * tok
    extra = rows_ref[...].reshape(count, LANES)[:, part : part + 3 * top]
    eye = (
        lax.broadcasted_iota(I32, (3 * top, 3 * top), 0) == lax.broadcasted_iota(I32, (3 * top, 3 * top), 1)
    ).astype(BF16)
    extra = lax.dot_general(eye, extra, (((1,), (1,)), ((), ())), preferred_element_type=F32)
    j = lax.broadcasted_iota(I32, (8, count), 0)
    z_count = 2 * lax.axis_size(FAR)
    expert = (((j // 2 % 2) * z_count + lax.axis_index(FAR) * 2 + j % 2) * 2 + j // 4).astype(F32)
    chosen = jnp.zeros((8, count), F32)
    gate = jnp.zeros((8, count), F32)
    for k in range(top):
        same = extra[k : k + 1] == expert
        chosen = jnp.where(same, 1.0, chosen)
        value = extra[top + k : top + k + 1] + extra[2 * top + k : 2 * top + k + 1]
        gate = gate + jnp.where(same, value, 0.0)
    first = lax.broadcasted_iota(I32, (count, count), 0)
    second = lax.broadcasted_iota(I32, (count, count), 1)
    before = ((first < second) & (first // tok == second // tok)).astype(BF16)
    place = jnp.dot(chosen.astype(BF16), before, preferred_element_type=F32)
    block = (lax.broadcasted_iota(I32, (8, count), 1) // tok).astype(F32)
    slot = jnp.where(chosen > 0.0, place + block * CAP, -1.0)
    want = lax.broadcasted_iota(I32, (8, blocks * CAP, count), 1).astype(F32)
    return slot[:, None, :] == want, gate


def pick_body(part, top, rows_ref, out_ref):
    near, half, _ = out_ref.shape
    near = near // 2
    hit, _ = slots_of(part, top, rows_ref)
    picker = jnp.where(hit, 1.0, 0.0).astype(BF16)
    rows = rows_ref[...].reshape(-1, LANES)[:, :part]
    sides = []
    for i in range(2):
        left = picker[:, i * half : (i + 1) * half].reshape(near * half, -1)
        sides.append(jnp.dot(left, rows, preferred_element_type=F32))
    got = jnp.concatenate(sides, axis=1).astype(BF16).reshape(near, half, 2 * part)
    out_ref[:near] = got
    out_ref[near:] = got


def weight_body(part, top, rows_ref, out_ref):
    _, half, count = out_ref.shape
    hit, gate = slots_of(part, top, rows_ref)
    weight = jnp.where(hit, gate[:, None, :], 0.0)
    high = weight.astype(BF16)
    low = (weight - high.astype(F32)).astype(BF16)
    both = jnp.concatenate([high, low], axis=2)
    near = both.shape[0]
    for i in range(2):
        side = both[:, i * (both.shape[1] // 2) : (i + 1) * (both.shape[1] // 2)]
        out_ref[i] = side.reshape(half, count)


def two_sides(rows, part):
    rows = rows.reshape(-1, 2 * part)
    return jnp.concatenate([rows[:, :part], rows[:, part:]], axis=0)


def gate_up_body(n_nar, rows_ref, *rest):
    parts, out_ref = [rest[ORDER.index(k)] for k in range(n_nar)], rest[-1]
    me = lax.axis_index("narrow")
    part = rows_ref.shape[2] // 2
    half = rows_ref.shape[0] // 2
    left = two_sides(rows_ref[:half], part)
    right = two_sides(rows_ref[half:], part)
    for k in range(n_nar):
        act = jnp.dot(left, parts[k][0], preferred_element_type=F32)
        act = act + jnp.dot(right, parts[k][1], preferred_element_type=F32)
        out_ref[place_of(lax.rem(me - k + n_nar, n_nar))] = act.astype(BF16)


def inner_body(acts_ref, out_ref):
    count, _, units = out_ref.shape
    act = sum(acts_ref[i].astype(F32) for i in range(count))
    gate, up = act[:, :units], act[:, units:]
    inner = (gate / (1.0 + jnp.exp(-gate)) * up).astype(BF16)
    for i in range(count):
        out_ref[i] = inner


def down_body(n_nar, inner_ref, *rest):
    parts, out_ref = [rest[ORDER.index(k)] for k in range(n_nar)], rest[-1]
    me = lax.axis_index("narrow")
    near = out_ref.shape[0] // 2
    units = inner_ref.shape[2]
    left = jnp.concatenate([inner_ref[place_of(lax.rem(me - k + n_nar, n_nar))] for k in range(n_nar)], axis=1)
    count = left.shape[0] // 2
    for i in range(2):
        right = jnp.concatenate([parts[k][2, :, i * units : (i + 1) * units] for k in range(n_nar)], axis=1)
        out = lax.dot_general(left, right, (((1,), (1,)), ((), ())), preferred_element_type=F32)
        out = jnp.concatenate([out[:count], out[count:]], axis=1).astype(BF16)
        out_ref[i * near : (i + 1) * near] = out.reshape(near, -1, out.shape[1])


def combine_body(rows_ref, weight_ref, out_ref):
    blocks, half, width = out_ref.shape
    near = rows_ref.shape[0] // 2
    part = width // 2
    total = 0.0
    for i in range(2):
        rows = rows_ref[i * near : (i + 1) * near].reshape(-1, width)
        for h in range(2):
            side = rows[:, h * part : (h + 1) * part]
            total = total + lax.dot_general(
                weight_ref[h], side, (((0,), (0,)), ((), ())), preferred_element_type=F32
            )
    count = total.shape[0] // 2
    total = (total[:count] + total[count:]).reshape(blocks, 2 * half, part)
    total = jnp.concatenate([total[:, :half], total[:, half:]], axis=2)
    out_ref[...] = total.astype(BF16)


def last_body(sums_ref, out_ref):
    total = sum(sums_ref[i].astype(F32) for i in range(sums_ref.shape[0]))
    half, width = total.shape
    out_ref[:half] = total[:, : width // 2].astype(BF16)
    out_ref[half:] = total[:, width // 2 :].astype(BF16)


def per_device(hidden, routes, route_gates, gate_proj, up_proj, down_proj):
    tok, width = hidden.shape
    top = routes.shape[1]
    n_grp, n_nar, n_far = lax.axis_size("grp"), lax.axis_size("narrow"), lax.axis_size(FAR)
    units = gate_proj.shape[2]
    part = width // (n_grp * n_nar)
    near = 16
    slots = 8 * n_far * CAP

    rows = call(
        functools.partial(rows_body, part, top),
        jax.ShapeDtypeStruct((n_far, tok, LANES), BF16),
        [HBM, HBM, HBM],
        [hidden, routes.T, route_gates.T],
        scratch=[
            pltpu.VMEM((tok, LANES), BF16),
            pltpu.VMEM((top, tok), I32),
            pltpu.VMEM((top, tok), F32),
            pltpu.SemaphoreType.DMA((3,)),
        ],
        mib=60,
    )
    rows = exchange(rows, FAR)

    parts = call(
        functools.partial(pack_body, n_nar, part),
        [jax.ShapeDtypeStruct((3, part, 2 * units), BF16)] * n_nar,
        [HBM, HBM, HBM],
        [gate_proj, up_proj, down_proj],
        place=HBM,
        scratch=[
            pltpu.VMEM((units, width), BF16),
            pltpu.VMEM((width, units), BF16),
            pltpu.VMEM((n_nar, 3, part, 2 * units), BF16),
            pltpu.SemaphoreType.DMA((n_nar, 2, 2)),
            pltpu.SemaphoreType.DMA((n_nar,)),
            pltpu.SemaphoreType.DMA((n_nar,)),
            pltpu.SemaphoreType.DMA,
        ],
        mib=60,
    )
    parts = [parts[ORDER.index(k)] for k in range(n_nar)]
    for k in ORDER[:-1]:
        parts[k] = lax.ppermute(parts[k], "narrow", [(i, (i + k) % n_nar) for i in range(n_nar)])
    half = n_far * CAP // 2
    picked = call(
        functools.partial(pick_body, part, top),
        jax.ShapeDtypeStruct((near, half, 2 * part), BF16),
        [VMEM],
        [rows],
        flops=2 * slots * n_far * tok * part,
    )
    weight = call(
        functools.partial(weight_body, part, top),
        jax.ShapeDtypeStruct((2, slots // 2, 2 * n_far * tok), BF16),
        [VMEM],
        [rows],
    )
    parts[0] = call(
        own_body,
        jax.ShapeDtypeStruct(parts[0].shape, BF16),
        [HBM, ANY],
        [parts[0], picked],
        scratch=[pltpu.SemaphoreType.DMA],
    )
    arrived = call(
        arrived_body, jax.ShapeDtypeStruct((8, 128), F32), [ANY] * n_nar, [parts[k] for k in ORDER], flops=HOLD
    )
    rows = exchange(picked, NEAR)

    acts = call(
        functools.partial(gate_up_body, n_nar),
        jax.ShapeDtypeStruct((n_nar, slots, 2 * units), BF16),
        [VMEM] + [VMEM] * n_nar + [ANY],
        [rows] + [parts[k] for k in ORDER] + [arrived],
        flops=2 * slots * part * 2 * units * 2 * n_nar,
    )
    acts = exchange(acts, "narrow")
    inner = call(inner_body, jax.ShapeDtypeStruct((n_nar, slots, units), BF16), [VMEM], [acts])
    inner = exchange(inner, "narrow")
    outs = call(
        functools.partial(down_body, n_nar),
        jax.ShapeDtypeStruct((near, half, 2 * part), BF16),
        [VMEM] + [VMEM] * n_nar,
        [inner] + [parts[k] for k in ORDER],
        flops=2 * slots * units * n_nar * 2 * part,
    )
    outs = exchange(outs, NEAR)
    sums = call(
        combine_body,
        jax.ShapeDtypeStruct((n_far, tok // 2, 2 * part), BF16),
        [VMEM, VMEM],
        [outs, weight],
        flops=2 * slots * 2 * 2 * n_far * tok * part,
    )
    sums = exchange(sums, FAR)
    return call(last_body, jax.ShapeDtypeStruct((tok, part), BF16), [VMEM], [sums])


def solution(mesh):
    n_grp, n_wide, n_nar = mesh.devices.shape
    fine = Mesh(mesh.devices.reshape(n_grp, 2, n_wide // 8, 2, 2, n_nar), AXES)
    return jax.shard_map(
        per_device,
        mesh=fine,
        in_specs=(
            P(WIDE, None),
            P(WIDE, None),
            P(WIDE, None),
            P(WIDE, None, ("grp", "narrow")),
            P(WIDE, None, ("grp", "narrow")),
            P(WIDE, ("grp", "narrow"), None),
        ),
        out_specs=P(WIDE, ("grp", "narrow")),
        check_vma=False,
    )
```
